128 devices in a mesh: loop: 16 (over x_lo, z, core), slab: 8 (over y, x_hi).
Axes of the slice: x: 4 (x_hi: 2, x_lo: 2; x = x_hi * 2 + x_lo), y: 4, z: 4, core: 2. Of those that a mesh axis runs over, the one named last changes fastest.
Arguments:
- signal: bfloat16 [32, 64, 64, 1920], P('slab', 'loop'), may hold values from -6 to 6
- width_class: int32 [32, 64, 64], P('slab', 'loop'), may hold values from 0 to 3
- kernel: float32 [3, 4], replicated, may hold values from 0.04 to 0.16
- taps: float32 [9], replicated, may hold values from 0.05 to 0.4
- chosen: int32 [16, 8, 512], P('loop', 'slab'), may hold values from 0 to 1023, as said below
Outputs:
- tiles: bfloat16 [8192, 8, 8192], P('loop', 'slab')
The draws below stay inside these ranges and needn't reach their ends.
Inputs may be any that keep to these rules, and one draw needn't show every extreme that they name: `chosen`: within one device the entries are distinct; 0 and 1023 occur on every device.
All inputs are finite; a program needn't handle non-finite values.
Results may differ from the reference program's by a relative error of at most 0.004.
Values may be sent and summed in bfloat16 or wider, within the bound.
A program may use at most 128 MiB of HBM per device.

```python
import jax
import jax.numpy as jnp
from jax import lax

CX = 4
CY = 4
CZ = 64
FRAMES = 1920
TAPS = 9
CLASSES = 4
PANEL = 512
VOX_DEV = 1024
NX = 32
NY = 64
N_LOOP = 16
N_SLAB = 8


def signal_field(key, base_lo, base_hi):
    first, second = jax.random.split(key)
    noise = jax.random.normal(first, (NX, NY, CZ, FRAMES), jnp.float32)
    base = jax.random.uniform(second, (NX, NY, CZ, 1), jnp.float32, base_lo, base_hi)
    return jnp.clip(noise + base, -6.0, 6.0)


def draw_signal(key, part):
    key = jax.random.fold_in(key, 11)
    values = signal_field(key, 1.5, 3.0)
    return values.astype(jnp.bfloat16)


def draw_chosen(key, part):
    key = jax.random.fold_in(key, 7)
    keys = jax.random.split(key, N_LOOP * N_SLAB)

    def single(each):
        first, second = jax.random.split(each)
        inner = jax.random.permutation(first, VOX_DEV - 2)[:PANEL - 2] + 1
        picks = jnp.concatenate([jnp.array([0, VOX_DEV - 1], jnp.int32), inner.astype(jnp.int32)])
        order = jax.random.permutation(second, PANEL)
        return picks[order].astype(jnp.int32)
    return jax.vmap(single)(keys).reshape(N_LOOP, N_SLAB, PANEL)


def set_ends(values, own_key, low, top_value):
    dims = values.shape
    index_at = [jax.random.randint(jax.random.fold_in(own_key, axis), (), 0, dims[axis]) for axis in range(len(dims))]
    values = values.at[tuple(index_at)].set(low)
    longest = dims.index(max(dims))
    index_at[longest] = (index_at[longest] + 1) % dims[longest]
    return values.at[tuple(index_at)].set(top_value)


def setup_inputs(seed: int = 0) -> dict:
    key_list = jax.random.split(jax.random.key(seed), 6)
    return {
        "signal": draw_signal(jax.random.fold_in(key_list[5], 71), 0),
        "width_class": set_ends(jax.random.randint(key_list[1], (NX, NY, CZ), 0, CLASSES), jax.random.fold_in(key_list[1], 1), 0, CLASSES - 1).astype(jnp.int32),
        "kernel": jnp.clip(jax.random.uniform(key_list[2], (3, CLASSES), jnp.float32, 0.04, 0.16), 0.04, 0.16),
        "taps": jnp.clip(jax.random.uniform(key_list[3], (TAPS,), jnp.float32, 0.05, 0.4), 0.05, 0.4),
        "chosen": draw_chosen(jax.random.fold_in(key_list[5], 71), 0),
    }


def smooth_block(padded, weights):
    center = padded[1:-1, 1:-1]
    along_x = padded[2:, 1:-1] + padded[:-2, 1:-1]
    along_y = padded[1:-1, 2:] + padded[1:-1, :-2]
    zpad = jnp.pad(center, ((0, 0), (0, 0), (1, 1), (0, 0)))
    along_z = zpad[:, :, 2:] + zpad[:, :, :-2]
    twice = 2.0 * center
    return center + weights[..., 0:1] * (along_x - twice) + weights[..., 1:2] * (along_y - twice) + weights[..., 2:3] * (along_z - twice)

def filter_norm(smoothed, taps):
    count = taps.shape[0]
    half = (count - 1) // 2
    frames = smoothed.shape[-1]
    padded = jnp.pad(smoothed, ((0, 0), (0, 0), (0, 0), (half, half)))
    filtered = jnp.zeros_like(smoothed)
    for step in range(count):
        filtered = filtered + taps[step] * padded[..., step:step + frames]
    centered = filtered - lax.optimization_barrier(jnp.mean(filtered, axis=-1, keepdims=True))
    scale = lax.rsqrt(lax.optimization_barrier(jnp.mean(centered * centered, axis=-1, keepdims=True)) + 1e-05)
    return (centered * scale).astype(jnp.bfloat16)

def lookup(width_class, kernel):
    weights = jnp.zeros(width_class.shape + (3,), jnp.float32)
    for klass in range(kernel.shape[1]):
        hit = (width_class == klass).astype(jnp.float32)[..., None]
        weights = weights + hit * kernel[:, klass]
    return weights

def reference(signal, width_class, kernel, taps, chosen):
    padded_all = jnp.pad(signal, ((1, 1), (1, 1), (0, 0), (0, 0)))
    blocks = []
    for slab in range(N_SLAB):
        part = padded_all[slab * CX:slab * CX + CX + 2].astype(jnp.float32)
        weights = lookup(width_class[slab * CX:slab * CX + CX], kernel)
        blocks.append(filter_norm(smooth_block(part, weights), taps))
    zscored = jnp.concatenate(blocks, axis=0)
    share = PANEL // N_SLAB
    picks = chosen.reshape(N_LOOP, N_SLAB, N_SLAB, share).transpose(0, 2, 1, 3)
    source = jnp.arange(N_SLAB, dtype=jnp.int32).reshape(1, 1, N_SLAB, 1)
    cycle = jnp.arange(N_LOOP, dtype=jnp.int32).reshape(N_LOOP, 1, 1, 1)
    xpos = source * CX + picks // (CY * CZ)
    ypos = cycle * CY + picks // CZ % CY
    zpos = picks % CZ
    panels = zscored[xpos, ypos, zpos]
    panels = panels.reshape(N_LOOP, N_SLAB, PANEL, FRAMES).transpose(1, 0, 2, 3).reshape(N_SLAB, N_LOOP * PANEL, FRAMES)
    inverse = 1.0 / FRAMES ** 0.5

    def one_group(group):
        wide = group.astype(jnp.float32)
        return (jnp.dot(wide, wide.T, preferred_element_type=jnp.float32) * inverse).astype(jnp.bfloat16)
    result = lax.map(one_group, panels)
    return result.transpose(1, 0, 2)
```

```python
import functools

import jax
import jax.numpy as jnp
from jax import lax
from jax.experimental import pallas as pl
from jax.experimental.pallas import tpu as pltpu
from jax.sharding import PartitionSpec as P

MESH = pl.DeviceIdType.MESH
CX, CY, CZ, FRAMES = 4, 4, 64, 1920
VOXELS = CX * CY * CZ
PANEL = 512
SHARE = 64
N_LOOP, N_SLAB = 16, 8
CHUNK = 384
CHUNKS = FRAMES // CHUNK
ORDER = (0, 1, 3, 2)


def front_kernel(sig, chosen, wclass, kernel, taps, rows, block, halo, vox, w_hi, w_lo, smooth, filt, load_sem, send_sem, recv_sem):
    loop, slab = lax.axis_index("loop"), lax.axis_index("slab")
    has = (slab > 0, slab < N_SLAB - 1, loop > 0, loop < N_LOOP - 1)
    peers = ((loop, slab - 1), (loop, slab + 1), (loop - 1, slab), (loop + 1, slab))
    planes = (sig.at[0], sig.at[CX - 1], sig.at[:, 0], sig.at[:, CY - 1])
    lands = (1, 0, 3, 2)

    barrier = pltpu.get_barrier_semaphore()
    for there, peer in zip(has, peers):
        @pl.when(there)
        def _():
            pl.semaphore_signal(barrier, inc=1, device_id=peer, device_id_type=MESH)
    load = pltpu.make_async_copy(sig, block, load_sem)
    load.start()
    pl.semaphore_wait(barrier, sum(there.astype(jnp.int32) for there in has))

    def halo_copy(d, k):
        lanes = pl.ds(k * CHUNK, CHUNK)
        return pltpu.make_async_remote_copy(
            src_ref=planes[d].at[:, :, lanes],
            dst_ref=halo.at[lands[d], :, :, lanes],
            send_sem=send_sem.at[d, k],
            recv_sem=recv_sem.at[lands[d], k],
            device_id=peers[d],
            device_id_type=MESH,
        )

    def halo_wait(d, k):
        lanes = pl.ds(k * CHUNK, CHUNK)
        pltpu.make_async_remote_copy(
            src_ref=halo.at[d, :, :, lanes],
            dst_ref=halo.at[d, :, :, lanes],
            send_sem=send_sem.at[d, k],
            recv_sem=recv_sem.at[d, k],
            device_id=peers[d],
            device_id_type=MESH,
        ).wait_recv()

    for k in range(CHUNKS):
        for d in range(4):
            @pl.when(has[d])
            def _():
                halo_copy(d, k).start()

    for d in range(4):
        @pl.when(jnp.logical_not(has[d]))
        def _():
            halo[d] = jnp.zeros_like(halo[d])
    pad = jnp.zeros((PANEL, 128), jnp.float32)
    smooth[:, 0:128] = pad
    smooth[:, 128 + FRAMES :] = pad

    index = jnp.broadcast_to(chosen[...].astype(jnp.float32), (128, PANEL))
    vox[...] = jnp.transpose(index).astype(jnp.int32)
    tall = 64

    def build(t, _):
        at = pl.ds(pl.multiple_of(t * tall, tall), tall)
        v = vox[at, :]
        iota = lax.broadcasted_iota(jnp.int32, (tall, 128), 1)
        iota_z = lax.broadcasted_iota(jnp.int32, (tall, CZ), 1)
        hits = jnp.zeros((tall, CZ), jnp.int32)
        for run in range(CX * CY):
            hits = hits + jnp.where(v[:, :CZ] == iota_z + run * CZ, wclass[run : run + 1, :], 0)
        klass = jnp.sum(hits.astype(jnp.float32), axis=1, keepdims=True)
        weight = []
        for d in range(3):
            w = jnp.zeros_like(klass)
            for c in range(4):
                w = w + jnp.where(klass == float(c), kernel[d, c], 0.0)
            weight.append(jnp.broadcast_to(w, (tall, 128)))
        wx, wy, wz = weight
        centre = 1.0 - 2.0 * (wx + wy + wz)
        x, y, z = v >> 8, (v >> 6) & 3, v & 63
        none = jnp.full_like(v, -1)
        y_lo, y_hi = jnp.where(y > 0, v - CZ, none), jnp.where(y < CY - 1, v + CZ, none)
        z_lo, z_hi = jnp.where(z > 0, v - 1, none), jnp.where(z < CZ - 1, v + 1, none)
        plane = x * CZ + z

        def put(column, w):
            hi = w.astype(jnp.bfloat16)
            w_hi[at, column : column + 128] = hi
            w_lo[at, column : column + 128] = (w - hi.astype(jnp.float32)).astype(jnp.bfloat16)

        zero = jnp.zeros((tall, 128), jnp.float32)
        for b in range(VOXELS // 128):
            col = iota + b * 128
            w = jnp.where(col == v, centre, zero)
            w = jnp.where((col == v - 256) | (col == v + 256), wx, w)
            w = jnp.where((col == y_lo) | (col == y_hi), wy, w)
            put(b * 128, jnp.where((col == z_lo) | (col == z_hi), wz, w))
        picks = (
            (v, wx),
            (v - 768, wx),
            (jnp.where(y == 0, plane, none), wy),
            (jnp.where(y == CY - 1, plane, none), wy),
        )
        for d, (pick, w) in enumerate(picks):
            for b in range(2):
                put(VOXELS + d * 256 + b * 128, jnp.where(iota + b * 128 == pick, w, zero))
        return 0

    lax.fori_loop(0, PANEL // tall, build, 0)

    half = 256

    def product(ref, first, k, h):
        at = pl.ds(pl.multiple_of(h * half, half), half)
        lanes = pl.ds(pl.multiple_of(k * CHUNK, 128), CHUNK)
        right = ref[:, :, :, lanes].reshape(VOXELS, CHUNK)
        cols = pl.ds(first, VOXELS)
        return jnp.dot(w_hi[at, cols], right, preferred_element_type=jnp.float32) + jnp.dot(
            w_lo[at, cols], right, preferred_element_type=jnp.float32
        )

    load.wait()

    def inner(i, _):
        k, h = i // 2, i % 2
        at = pl.ds(pl.multiple_of(h * half, half), half)
        smooth[at, pl.ds(pl.multiple_of(128 + k * CHUNK, 128), CHUNK)] = product(block, 0, k, h)
        return 0

    lax.fori_loop(0, CHUNKS * 2, inner, 0)

    def filter_part(first, width):
        def body(t, _):
            at = pl.ds(pl.multiple_of(t * 16, 16), 16)
            window = smooth[at, pl.ds(first, width + 256)]
            total = None
            for tap in range(9):
                shift = 4 - tap
                moved = window if shift == 0 else pltpu.roll(window, shift % (width + 256), axis=1)
                term = taps[tap] * moved[:, 128 : 128 + width]
                total = term if total is None else total + term
            filt[at, pl.ds(first, width)] = total
            return 0

        lax.fori_loop(0, PANEL // 16, body, 0)

    for k in range(CHUNKS):
        for d in range(4):
            @pl.when(has[d])
            def _():
                halo_wait(d, k)

        def outer(h, _):
            at = pl.ds(pl.multiple_of(h * half, half), half)
            smooth[at, 128 + k * CHUNK : 128 + (k + 1) * CHUNK] += product(halo, VOXELS, k, h)
            return 0

        lax.fori_loop(0, 2, outer, 0)
        first = max(0, k * CHUNK - 128)
        last = FRAMES if k == CHUNKS - 1 else (k + 1) * CHUNK - 128
        filter_part(first, last - first)

    def norm(t, _):
        at = pl.ds(pl.multiple_of(t * 16, 16), 16)
        f = filt[at, :]
        centred = f - jnp.mean(f, axis=1, keepdims=True)
        scale = lax.rsqrt(jnp.mean(centred * centred, axis=1, keepdims=True) + 1e-05)
        rows[at, :] = (centred * scale).astype(jnp.bfloat16)
        return 0

    lax.fori_loop(0, PANEL // 16, norm, 0)

    for k in range(CHUNKS):
        for d in range(4):
            @pl.when(has[d])
            def _():
                halo_copy(d, k).wait_send()


def front(signal, chosen, wclass, kernel, taps):
    vmem = pl.BlockSpec(memory_space=pltpu.VMEM)
    smem = pl.BlockSpec(memory_space=pltpu.SMEM)
    return pl.pallas_call(
        front_kernel,
        out_shape=jax.ShapeDtypeStruct((PANEL, FRAMES), jnp.bfloat16),
        in_specs=[pl.BlockSpec(memory_space=pl.ANY), vmem, vmem, smem, smem],
        out_specs=vmem,
        scratch_shapes=[
            pltpu.VMEM((CX, CY, CZ, FRAMES), jnp.bfloat16),
            pltpu.VMEM((4, 4, CZ, FRAMES), jnp.bfloat16),
            pltpu.VMEM((PANEL, 128), jnp.int32),
            pltpu.VMEM((PANEL, 2 * VOXELS), jnp.bfloat16),
            pltpu.VMEM((PANEL, 2 * VOXELS), jnp.bfloat16),
            pltpu.VMEM((PANEL, FRAMES + 256), jnp.float32),
            pltpu.VMEM((PANEL, FRAMES), jnp.float32),
            pltpu.SemaphoreType.DMA,
            pltpu.SemaphoreType.DMA((4, CHUNKS)),
            pltpu.SemaphoreType.DMA((4, CHUNKS)),
        ],
        compiler_params=pltpu.CompilerParams(
            collective_id=0, has_side_effects=True, vmem_limit_bytes=56 * 2**20
        ),
        name="front",
    )(signal, chosen, wclass, kernel, taps)


def group_kernel(rows, tiles, held, stage, own_sem, swap_sem, x_sem, up_sem, down_sem, core_sem, recv_sem, out_sem):
    loop, slab = lax.axis_index("loop"), lax.axis_index("slab")
    x, z, c = loop // 8, (loop // 2) % 4, loop % 2
    y, h = slab // 2, slab % 2
    z_up, z_down, z_far = (z + 1) % 4, (z + 3) % 4, (z + 2) % 4

    def panel(px, pz, pc=None):
        return px * 8 + pz * 2 + (c if pc is None else pc)

    up, down = (panel(x, z_up), slab), (panel(x, z_down), slab)
    across, sibling = (panel(1 - x, z), slab), (panel(x, z, 1 - c), slab)
    inside = [(loop, ((y + dy) % 4) * 2 + h) for dy in (1, 3, 2)]
    outside = [(panel(1 - x, z), ((y + dy) % 4) * 2 + 1 - h) for dy in ORDER]

    barrier = pltpu.get_barrier_semaphore()
    peers = [up, down, across, sibling] + inside + outside
    for peer in peers:
        pl.semaphore_signal(barrier, inc=1, device_id=peer, device_id_type=MESH)
    pl.semaphore_wait(barrier, len(peers))

    def at(p):
        dy = jnp.where(p == 2, 3, jnp.where(p == 3, 2, p))
        return (y + dy) % 4

    def copy(q, py, ph, sem, peer):
        return pltpu.make_async_remote_copy(
            src_ref=held.at[q, py, ph],
            dst_ref=held.at[q, py, ph],
            send_sem=sem.at[q, py, ph],
            recv_sem=recv_sem.at[q, py, ph],
            device_id=peer,
            device_id_type=MESH,
        )

    def arrived(q, py, ph):
        copy(q, py, ph, core_sem, sibling).wait_recv()

    swaps = []
    for i, peer in enumerate(outside + inside):
        to_y, to_h = peer[1] // 2, peer[1] % 2
        swaps.append(pltpu.make_async_remote_copy(
            src_ref=rows.at[to_y, to_h],
            dst_ref=held.at[loop, y, h],
            send_sem=swap_sem.at[i],
            recv_sem=recv_sem.at[loop, y, h],
            device_id=peer,
            device_id_type=MESH,
        ))
    pltpu.make_async_copy(rows.at[y, h], held.at[loop, y, h], recv_sem.at[loop, y, h]).start()
    for i in (0, 4, 1, 5, 2, 6, 3):
        swaps[i].start()

    mine, other = panel(x, z), panel(1 - x, z)

    def begin(p, _):
        py = at(p)

        @pl.when(p == 0)
        def _():
            pltpu.make_async_copy(rows.at[y, h], held.at[loop, y, h], recv_sem.at[loop, y, h]).wait()

        @pl.when(p > 0)
        def _():
            arrived(mine, py, h)
        copy(mine, py, h, up_sem, up).start()
        copy(mine, py, h, down_sem, down).start()
        copy(mine, py, h, x_sem, across).start()
        copy(mine, py, h, core_sem, sibling).start()
        arrived(other, py, 1 - h)
        copy(other, py, 1 - h, x_sem, across).start()
        copy(other, py, 1 - h, up_sem, up).start()
        copy(other, py, 1 - h, down_sem, down).start()
        copy(other, py, 1 - h, core_sem, sibling).start()
        return 0

    lax.fori_loop(0, 4, begin, 0)

    def second(p, _):
        py = at(p)
        even = p % 2 == 0
        for pz, sem, peer, on in ((z_down, up_sem, up, even), (z_up, down_sem, down, jnp.logical_not(even))):
            for px, ph in ((x, h), (1 - x, 1 - h)):
                q = panel(px, pz)
                arrived(q, py, ph)

                @pl.when(on)
                def _():
                    copy(q, py, ph, sem, peer).start()
                if px is x:
                    copy(q, py, ph, x_sem, across).start()
                copy(q, py, ph, core_sem, sibling).start()
        arrived(mine, py, 1 - h)
        copy(mine, py, 1 - h, up_sem, up).start()
        copy(mine, py, 1 - h, down_sem, down).start()
        copy(mine, py, 1 - h, core_sem, sibling).start()
        arrived(other, py, h)
        copy(other, py, h, core_sem, sibling).start()
        return 0

    lax.fori_loop(0, 4, second, 0)

    def from_sibling(px, pz):
        def body(i, _):
            arrived(panel(px, pz, 1 - c), i // 2, i % 2)
            return 0

        lax.fori_loop(0, 8, body, 0)

    def tile(q):
        left = held[loop].reshape(PANEL, FRAMES)
        for j in range(2):
            right = held[q, 2 * j : 2 * j + 2].reshape(PANEL // 2, FRAMES)
            product = lax.dot_general(left, right, (((1,), (1,)), ((), ())), preferred_element_type=jnp.float32)
            stage[q, :, j * 256 : (j + 1) * 256] = (product * (1.0 / FRAMES**0.5)).astype(jnp.bfloat16)
        tile_copy(q).start()

    def tile_copy(q):
        return pltpu.make_async_copy(
            stage.at[q], tiles.at[:, pl.ds(pl.multiple_of(q * PANEL, PANEL), PANEL)], out_sem.at[q]
        )

    def both(px, pz):
        from_sibling(px, pz)

        def body(pc, _):
            tile(panel(px, pz, pc))
            return 0

        lax.fori_loop(0, 2, body, 0)

    def third(p, _):
        py = at(p)
        q = panel(x, z_far)
        arrived(q, py, h)
        copy(q, py, h, x_sem, across).start()
        copy(q, py, h, core_sem, sibling).start()
        even = p % 2 == 0
        for pz, sem, peer, on in ((z_down, up_sem, up, even), (z_up, down_sem, down, jnp.logical_not(even))):
            q = panel(x, pz)
            arrived(q, py, 1 - h)

            @pl.when(on)
            def _():
                copy(q, py, 1 - h, sem, peer).start()
            copy(q, py, 1 - h, core_sem, sibling).start()
        q = panel(1 - x, z_far)
        arrived(q, py, 1 - h)
        copy(q, py, 1 - h, core_sem, sibling).start()
        return 0

    lax.fori_loop(0, 4, third, 0)

    def near(i, _):
        both(jnp.where(i == 0, x, 1 - x), z)
        return 0

    lax.fori_loop(0, 2, near, 0)

    def fourth(p, _):
        py = at(p)
        for pz in (z_down, z_up):
            q = panel(1 - x, pz)
            arrived(q, py, h)
            copy(q, py, h, core_sem, sibling).start()
        return 0

    lax.fori_loop(0, 4, fourth, 0)

    def beside(i, _):
        both(x, jnp.where(i == 0, z_down, z_up))
        return 0

    lax.fori_loop(0, 2, beside, 0)

    def fifth(p, _):
        py = at(p)
        q = panel(x, z_far)
        arrived(q, py, 1 - h)
        copy(q, py, 1 - h, core_sem, sibling).start()
        return 0

    lax.fori_loop(0, 4, fifth, 0)

    def beyond(i, _):
        both(jnp.where(i == 2, x, 1 - x), jnp.where(i == 0, z_down, jnp.where(i == 1, z_up, z_far)))
        return 0

    lax.fori_loop(0, 3, beyond, 0)

    def sixth(p, _):
        py = at(p)
        q = panel(1 - x, z_far)
        arrived(q, py, h)
        copy(q, py, h, core_sem, sibling).start()
        return 0

    lax.fori_loop(0, 4, sixth, 0)
    both(1 - x, z_far)

    for swap in swaps:
        swap.wait_send()

    def left(p, _):
        py = at(p)
        even = p % 2 == 0
        for pz in range(4):
            q = panel(x, pz)
            copy(q, py, h, x_sem, across).wait_send()
            for px in range(2):
                for ph in range(2):
                    copy(panel(px, pz), py, ph, core_sem, sibling).wait_send()
        copy(other, py, 1 - h, x_sem, across).wait_send()
        for q, ph in ((mine, h), (other, 1 - h), (mine, 1 - h)):
            copy(q, py, ph, up_sem, up).wait_send()
            copy(q, py, ph, down_sem, down).wait_send()
        for px, ph in ((x, h), (1 - x, 1 - h), (x, 1 - h)):
            @pl.when(even)
            def _():
                copy(panel(px, z_down), py, ph, up_sem, up).wait_send()

            @pl.when(jnp.logical_not(even))
            def _():
                copy(panel(px, z_up), py, ph, down_sem, down).wait_send()
        return 0

    lax.fori_loop(0, 4, left, 0)

    def written(q, _):
        tile_copy(q).wait()
        return 0

    lax.fori_loop(0, N_LOOP, written, 0)


def group(rows):
    block = (N_LOOP, 4, 2)
    return pl.pallas_call(
        group_kernel,
        out_shape=jax.ShapeDtypeStruct((PANEL, N_LOOP * PANEL), jnp.bfloat16),
        in_specs=[pl.BlockSpec(memory_space=pltpu.VMEM)],
        out_specs=pl.BlockSpec(memory_space=pl.ANY),
        scratch_shapes=[
            pltpu.VMEM(block + (SHARE, FRAMES), jnp.bfloat16),
            pltpu.VMEM((N_LOOP, PANEL, PANEL), jnp.bfloat16),
            pltpu.SemaphoreType.DMA,
            pltpu.SemaphoreType.DMA((7,)),
            pltpu.SemaphoreType.DMA(block),
            pltpu.SemaphoreType.DMA(block),
            pltpu.SemaphoreType.DMA(block),
            pltpu.SemaphoreType.DMA(block),
            pltpu.SemaphoreType.DMA(block),
            pltpu.SemaphoreType.DMA((N_LOOP,)),
        ],
        compiler_params=pltpu.CompilerParams(
            collective_id=1, has_side_effects=True, vmem_limit_bytes=56 * 2**20
        ),
        name="group",
    )(rows)


def local(signal, width_class, kernel, taps, chosen):
    rows = front(signal, chosen.reshape(1, PANEL), width_class.reshape(CX * CY, CZ), kernel, taps)
    wide = group(rows.reshape(4, 2, SHARE, FRAMES))
    return wide.reshape(PANEL, 1, N_LOOP * PANEL)


def solution(mesh):
    in_specs = (
        P("slab", "loop", None, None),
        P("slab", "loop", None),
        P(),
        P(),
        P("loop", "slab", None),
    )
    return jax.shard_map(local, mesh=mesh, in_specs=in_specs, out_specs=P("loop", "slab", None), check_vma=False)
```

```python
import functools

import jax
import jax.numpy as jnp
from jax import lax
from jax.experimental import pallas as pl
from jax.experimental.pallas import tpu as pltpu
from jax.sharding import PartitionSpec as P

MESH = pl.DeviceIdType.MESH
CX, CY, CZ, FRAMES = 4, 4, 64, 1920
VOXELS = CX * CY * CZ
PANEL = 512
SHARE = 64
N_LOOP, N_SLAB = 16, 8
EDGES = (0, 384, 896, 1408, 1664, 1920)
CHUNKS = len(EDGES) - 1
WIDE = 384
REACH = 128
FILTER = 256
ORDER = (0, 1, 3, 2)


def front_kernel(sig, chosen, wclass, kernel, taps, rows, block, halo, vox, w_hi, w_lo, s_hi, s_lo, t_hi, t_lo, filt, sums, load_sem, send_sem, recv_sem):
    loop, slab = lax.axis_index("loop"), lax.axis_index("slab")
    has = (slab > 0, slab < N_SLAB - 1, loop > 0, loop < N_LOOP - 1)
    peers = ((loop, slab - 1), (loop, slab + 1), (loop - 1, slab), (loop + 1, slab))
    planes = (sig.at[0], sig.at[CX - 1], sig.at[:, 0], sig.at[:, CY - 1])
    lands = (1, 0, 3, 2)

    barrier = pltpu.get_barrier_semaphore()
    for there, peer in zip(has, peers):
        @pl.when(there)
        def _():
            pl.semaphore_signal(barrier, inc=1, device_id=peer, device_id_type=MESH)
    load = pltpu.make_async_copy(sig, block, load_sem)
    load.start()
    pl.semaphore_wait(barrier, sum(there.astype(jnp.int32) for there in has))

    def halo_copy(d, k):
        lanes = pl.ds(EDGES[k], EDGES[k + 1] - EDGES[k])
        return pltpu.make_async_remote_copy(
            src_ref=planes[d].at[:, :, lanes],
            dst_ref=halo.at[lands[d], :, :, lanes],
            send_sem=send_sem.at[d, k],
            recv_sem=recv_sem.at[lands[d], k],
            device_id=peers[d],
            device_id_type=MESH,
        )

    def halo_wait(d, k):
        lanes = pl.ds(EDGES[k], EDGES[k + 1] - EDGES[k])
        pltpu.make_async_remote_copy(
            src_ref=halo.at[d, :, :, lanes],
            dst_ref=halo.at[d, :, :, lanes],
            send_sem=send_sem.at[d, k],
            recv_sem=recv_sem.at[d, k],
            device_id=peers[d],
            device_id_type=MESH,
        ).wait_recv()

    for k in range(CHUNKS):
        for d in range(4):
            @pl.when(has[d])
            def _():
                halo_copy(d, k).start()

    for d in range(4):
        @pl.when(jnp.logical_not(has[d]))
        def _():
            halo[d] = jnp.zeros_like(halo[d])
    for part in (s_hi, s_lo):
        part[:, 0:REACH] = jnp.zeros((PANEL, REACH), jnp.bfloat16)
        part[:, REACH + FRAMES :] = jnp.zeros((PANEL, REACH), jnp.bfloat16)

    def split(value):
        hi = value.astype(jnp.bfloat16)
        return hi, (value - hi.astype(jnp.float32)).astype(jnp.bfloat16)

    wide = FILTER + 2 * REACH
    lag = lax.broadcasted_iota(jnp.int32, (wide, FILTER), 0) - lax.broadcasted_iota(jnp.int32, (wide, FILTER), 1) - REACH + 4
    band = jnp.zeros((wide, FILTER), jnp.float32)
    for tap in range(9):
        band = jnp.where(lag == tap, taps[tap], band)
    t_hi[...], t_lo[...] = split(band)

    index = jnp.broadcast_to(chosen[...].astype(jnp.float32), (128, PANEL))
    vox[...] = jnp.transpose(index).astype(jnp.int32)
    tall = 64

    def build(t, _):
        at = pl.ds(pl.multiple_of(t * tall, tall), tall)
        v = vox[at, :]
        iota = lax.broadcasted_iota(jnp.int32, (tall, 128), 1)
        iota_z = lax.broadcasted_iota(jnp.int32, (tall, CZ), 1)
        hits = jnp.zeros((tall, CZ), jnp.int32)
        for run in range(CX * CY):
            hits = hits + jnp.where(v[:, :CZ] == iota_z + run * CZ, wclass[run : run + 1, :], 0)
        klass = jnp.sum(hits.astype(jnp.float32), axis=1, keepdims=True)
        weight = []
        for d in range(3):
            w = jnp.zeros_like(klass)
            for c in range(4):
                w = w + jnp.where(klass == float(c), kernel[d, c], 0.0)
            weight.append(jnp.broadcast_to(w, (tall, 128)))
        wx, wy, wz = weight
        centre = 1.0 - 2.0 * (wx + wy + wz)
        x, y, z = v >> 8, (v >> 6) & 3, v & 63
        none = jnp.full_like(v, -1)
        y_lo, y_hi = jnp.where(y > 0, v - CZ, none), jnp.where(y < CY - 1, v + CZ, none)
        z_lo, z_hi = jnp.where(z > 0, v - 1, none), jnp.where(z < CZ - 1, v + 1, none)
        plane = x * CZ + z

        def put(column, w):
            w_hi[at, column : column + 128], w_lo[at, column : column + 128] = split(w)

        zero = jnp.zeros((tall, 128), jnp.float32)
        for b in range(VOXELS // 128):
            col = iota + b * 128
            w = jnp.where(col == v, centre, zero)
            w = jnp.where((col == v - 256) | (col == v + 256), wx, w)
            w = jnp.where((col == y_lo) | (col == y_hi), wy, w)
            put(b * 128, jnp.where((col == z_lo) | (col == z_hi), wz, w))
        picks = (
            (v, wx),
            (v - 768, wx),
            (jnp.where(y == 0, plane, none), wy),
            (jnp.where(y == CY - 1, plane, none), wy),
        )
        for d, (pick, w) in enumerate(picks):
            for b in range(2):
                put(VOXELS + d * 256 + b * 128, jnp.where(iota + b * 128 == pick, w, zero))
        return 0

    lax.fori_loop(0, PANEL // tall, build, 0)

    half = 256

    def product(ref, first, lanes, h):
        at = pl.ds(pl.multiple_of(h * half, half), half)
        right = ref[:, :, :, lanes].reshape(VOXELS, -1)
        cols = pl.ds(first, VOXELS)
        return jnp.dot(w_hi[at, cols], right, preferred_element_type=jnp.float32) + jnp.dot(
            w_lo[at, cols], right, preferred_element_type=jnp.float32
        )

    load.wait()

    def inner(i, _):
        k, h = i // 2, i % 2
        at = pl.ds(pl.multiple_of(h * half, half), half)
        lanes = pl.ds(pl.multiple_of(k * WIDE, 128), WIDE)
        filt[at, lanes] = product(block, 0, lanes, h)
        return 0

    lax.fori_loop(0, FRAMES // WIDE * 2, inner, 0)
    sums[...] = jnp.zeros_like(sums)

    def filter_part(at, first, width):
        window = pl.ds(first, width + 2 * REACH)
        hi, lo = s_hi[at, window], s_lo[at, window]
        rows_of = pl.ds(0, width + 2 * REACH)
        cols = pl.ds(0, width)
        a, b = t_hi[rows_of, cols], t_lo[rows_of, cols]
        total = jnp.dot(hi, a, preferred_element_type=jnp.float32)
        total = total + jnp.dot(hi, b, preferred_element_type=jnp.float32)
        total = total + jnp.dot(lo, a, preferred_element_type=jnp.float32)
        filt[at, pl.ds(first, width)] = total
        for i in range(width // 128):
            sums[at, :] += total[:, i * 128 : (i + 1) * 128]

    for k in range(CHUNKS):
        for d in range(4):
            @pl.when(has[d])
            def _():
                halo_wait(d, k)

        lanes = pl.ds(EDGES[k], EDGES[k + 1] - EDGES[k])
        shifted = pl.ds(EDGES[k] + REACH, EDGES[k + 1] - EDGES[k])
        first = max(0, EDGES[k] - REACH)
        last = FRAMES if k == CHUNKS - 1 else EDGES[k + 1] - REACH

        def outer(h, _):
            at = pl.ds(pl.multiple_of(h * half, half), half)
            s_hi[at, shifted], s_lo[at, shifted] = split(filt[at, lanes] + product(halo, VOXELS, lanes, h))
            for start in range(first, last, FILTER):
                filter_part(at, start, min(FILTER, last - start))
            return 0

        lax.fori_loop(0, 2, outer, 0)

    deep = 64

    def norm(t, _):
        at = pl.ds(pl.multiple_of(t * deep, deep), deep)
        mean = jnp.sum(sums[at, :], axis=1, keepdims=True) * (1.0 / FRAMES)
        wide_mean = jnp.broadcast_to(mean, (deep, 128))
        square = jnp.zeros((deep, 128), jnp.float32)
        for i in range(FRAMES // 128):
            centred = filt[at, i * 128 : (i + 1) * 128] - wide_mean
            square = square + centred * centred
        scale = lax.rsqrt(jnp.sum(square, axis=1, keepdims=True) * (1.0 / FRAMES) + 1e-05)
        wide_scale = jnp.broadcast_to(scale, (deep, 128))
        for i in range(FRAMES // 128):
            lanes = slice(i * 128, (i + 1) * 128)
            rows[at, lanes] = ((filt[at, lanes] - wide_mean) * wide_scale).astype(jnp.bfloat16)
        return 0

    lax.fori_loop(0, PANEL // deep, norm, 0)

    for k in range(CHUNKS):
        for d in range(4):
            @pl.when(has[d])
            def _():
                halo_copy(d, k).wait_send()


def front(signal, chosen, wclass, kernel, taps):
    vmem = pl.BlockSpec(memory_space=pltpu.VMEM)
    smem = pl.BlockSpec(memory_space=pltpu.SMEM)
    return pl.pallas_call(
        front_kernel,
        out_shape=jax.ShapeDtypeStruct((PANEL, FRAMES), jnp.bfloat16),
        in_specs=[pl.BlockSpec(memory_space=pl.ANY), vmem, vmem, smem, smem],
        out_specs=vmem,
        scratch_shapes=[
            pltpu.VMEM((CX, CY, CZ, FRAMES), jnp.bfloat16),
            pltpu.VMEM((4, 4, CZ, FRAMES), jnp.bfloat16),
            pltpu.VMEM((PANEL, 128), jnp.int32),
            pltpu.VMEM((PANEL, 2 * VOXELS), jnp.bfloat16),
            pltpu.VMEM((PANEL, 2 * VOXELS), jnp.bfloat16),
            pltpu.VMEM((PANEL, FRAMES + 2 * REACH), jnp.bfloat16),
            pltpu.VMEM((PANEL, FRAMES + 2 * REACH), jnp.bfloat16),
            pltpu.VMEM((FILTER + 2 * REACH, FILTER), jnp.bfloat16),
            pltpu.VMEM((FILTER + 2 * REACH, FILTER), jnp.bfloat16),
            pltpu.VMEM((PANEL, FRAMES), jnp.float32),
            pltpu.VMEM((PANEL, 128), jnp.float32),
            pltpu.SemaphoreType.DMA,
            pltpu.SemaphoreType.DMA((4, CHUNKS)),
            pltpu.SemaphoreType.DMA((4, CHUNKS)),
        ],
        compiler_params=pltpu.CompilerParams(
            collective_id=0, has_side_effects=True, vmem_limit_bytes=56 * 2**20
        ),
        name="front",
    )(signal, chosen, wclass, kernel, taps)


def group_kernel(rows, tiles, held, near_out, near_in, last_out, last_in, swap_sem, x_sem, up_sem, down_sem, core_sem, recv_sem, lend_sem, borrow_sem):
    loop, slab = lax.axis_index("loop"), lax.axis_index("slab")
    x, z, c = loop // 8, (loop // 2) % 4, loop % 2
    y, h = slab // 2, slab % 2
    z_up, z_down, z_far = (z + 1) % 4, (z + 3) % 4, (z + 2) % 4

    def panel(px, pz, pc=None):
        return px * 8 + pz * 2 + (c if pc is None else pc)

    up, down = (panel(x, z_up), slab), (panel(x, z_down), slab)
    across, sibling = (panel(1 - x, z), slab), (panel(x, z, 1 - c), slab)
    inside = [(loop, ((y + dy) % 4) * 2 + h) for dy in (1, 3, 2)]
    outside = [(panel(1 - x, z), ((y + dy) % 4) * 2 + 1 - h) for dy in ORDER]

    barrier = pltpu.get_barrier_semaphore()
    peers = [up, down, across, sibling] + inside + outside
    for peer in peers:
        pl.semaphore_signal(barrier, inc=1, device_id=peer, device_id_type=MESH)
    pl.semaphore_wait(barrier, len(peers))

    def at(p):
        dy = jnp.where(p == 2, 3, jnp.where(p == 3, 2, p))
        return (y + dy) % 4

    def copy(q, py, ph, sem, peer):
        return pltpu.make_async_remote_copy(
            src_ref=held.at[q, py, ph],
            dst_ref=held.at[q, py, ph],
            send_sem=sem.at[q, py, ph],
            recv_sem=recv_sem.at[q, py, ph],
            device_id=peer,
            device_id_type=MESH,
        )

    def arrived(q, py, ph):
        copy(q, py, ph, core_sem, sibling).wait_recv()

    swaps = []
    for i, peer in enumerate(outside + inside):
        to_y, to_h = peer[1] // 2, peer[1] % 2
        swaps.append(pltpu.make_async_remote_copy(
            src_ref=rows.at[to_y, to_h],
            dst_ref=held.at[loop, y, h],
            send_sem=swap_sem.at[i],
            recv_sem=recv_sem.at[loop, y, h],
            device_id=peer,
            device_id_type=MESH,
        ))
    pltpu.make_async_copy(rows.at[y, h], held.at[loop, y, h], recv_sem.at[loop, y, h]).start()
    for i in (0, 4, 1, 5, 2, 6, 3):
        swaps[i].start()

    mine, other = panel(x, z), panel(1 - x, z)
    y_last = (y + 2) % 4
    for pz in (z_down, z_up, z_far):
        for pc in range(2):
            held[panel(x, pz, pc), y_last, 1 - h] = jnp.zeros((SHARE, FRAMES), jnp.bfloat16)

    def begin(p, _):
        py = at(p)

        @pl.when(p == 0)
        def _():
            pltpu.make_async_copy(rows.at[y, h], held.at[loop, y, h], recv_sem.at[loop, y, h]).wait()

        @pl.when(p > 0)
        def _():
            arrived(mine, py, h)
        copy(mine, py, h, up_sem, up).start()
        copy(mine, py, h, down_sem, down).start()
        copy(mine, py, h, x_sem, across).start()
        copy(mine, py, h, core_sem, sibling).start()
        arrived(other, py, 1 - h)
        copy(other, py, 1 - h, x_sem, across).start()
        copy(other, py, 1 - h, up_sem, up).start()
        copy(other, py, 1 - h, down_sem, down).start()
        copy(other, py, 1 - h, core_sem, sibling).start()
        return 0

    lax.fori_loop(0, 4, begin, 0)

    def second(p, _):
        py = at(p)
        even = p % 2 == 0
        for pz, sem, peer, on in ((z_down, up_sem, up, even), (z_up, down_sem, down, jnp.logical_not(even))):
            for q, ph in ((panel(x, pz), h), (panel(1 - x, pz), 1 - h)):
                arrived(q, py, ph)

                @pl.when(on)
                def _():
                    copy(q, py, ph, sem, peer).start()
                copy(q, py, ph, core_sem, sibling).start()
        arrived(mine, py, 1 - h)

        @pl.when(p < 3)
        def _():
            copy(mine, py, 1 - h, up_sem, up).start()
            copy(mine, py, 1 - h, down_sem, down).start()
        copy(mine, py, 1 - h, core_sem, sibling).start()
        arrived(other, py, h)
        copy(other, py, h, core_sem, sibling).start()
        return 0

    lax.fori_loop(0, 4, second, 0)

    def from_sibling(px, pz, ph, count=4):
        def body(p, _):
            arrived(panel(px, pz, 1 - c), at(p), ph)
            return 0

        lax.fori_loop(0, count, body, 0)

    def times(q, right):
        left = held[q].reshape(PANEL, FRAMES)
        product = lax.dot_general(left, right, (((1,), (1,)), ((), ())), preferred_element_type=jnp.float32)
        return product * (1.0 / FRAMES**0.5)

    def lend(j, i):
        if i < 2:
            src, dst = near_out.at[j, i], near_in.at[j, i]
        else:
            src, dst = last_out.at[j], last_in.at[j]
        return pltpu.make_async_remote_copy(
            src_ref=src, dst_ref=dst, send_sem=lend_sem.at[j, i], recv_sem=borrow_sem.at[j, i], device_id=across, device_id_type=MESH
        )

    def compute_for_across(j, pz):
        from_sibling(x, pz, h)
        from_sibling(1 - x, pz, 1 - h)
        for pc in range(2):
            right = held[panel(x, pz, pc), :, h].reshape(PANEL // 2, FRAMES)
            near_out[j, pc] = times(other, right).astype(jnp.bfloat16)
            lend(j, pc).start()
        right = jnp.concatenate([held[panel(1 - x, pz, pc), y_last, 1 - h] for pc in range(2)], axis=0)
        last_out[j] = times(other, right).astype(jnp.bfloat16)
        lend(j, 2).start()

    def columns(q, first, width):
        return pl.ds(pl.multiple_of(q * PANEL + first, 128), width)

    def full(q):
        for j in range(2):
            right = held[q, 2 * j : 2 * j + 2].reshape(PANEL // 2, FRAMES)
            tiles[:, columns(q, j * 256, 256)] = times(loop, right).astype(jnp.bfloat16)

    def whole(px):
        from_sibling(px, z, 0)
        from_sibling(px, z, 1)

        def body(pc, _):
            q = panel(px, z, pc)
            full(q)
            return 0

        lax.fori_loop(0, 2, body, 0)

    lane = lax.broadcasted_iota(jnp.int32, (PANEL, 128), 1)

    def same_column(j, pz):
        from_sibling(x, pz, 1 - h, 3)
        lend(j, 2).wait_recv()

        def body(pc, _):
            q = panel(x, pz, pc)
            full(q)
            part = last_in[j].astype(jnp.float32)
            part = jnp.where(pc == 1 - h, part, pltpu.roll(part, 64, axis=1))
            place = columns(q, y_last * 128, 128)
            keep = tiles[:, place].astype(jnp.float32)
            tiles[:, place] = jnp.where(lane // 64 == 1 - h, part, keep).astype(jnp.bfloat16)
            return 0

        lax.fori_loop(0, 2, body, 0)

    def other_column(j, pz):
        for pc in range(2):
            lend(j, pc).wait_recv()

        def body(pc, _):
            q = panel(1 - x, pz, pc)
            here = times(loop, held[q, :, 1 - h].reshape(PANEL // 2, FRAMES))
            there = near_in[j, pc].astype(jnp.float32)
            low, high = jnp.where(h == 0, there, here), jnp.where(h == 0, here, there)
            for i in range(2):
                a, b = low[:, i * 128 : (i + 1) * 128], high[:, i * 128 : (i + 1) * 128]
                first = jnp.where(lane < 64, a, pltpu.roll(b, 64, axis=1))
                after = jnp.where(lane < 64, pltpu.roll(a, 64, axis=1), b)
                tiles[:, columns(q, i * 256, 128)] = first.astype(jnp.bfloat16)
                tiles[:, columns(q, i * 256 + 128, 128)] = after.astype(jnp.bfloat16)
            return 0

        lax.fori_loop(0, 2, body, 0)

    def beside(body):
        def step(j, _):
            body(j, jnp.where(j == 0, z_down, z_up))
            return 0

        lax.fori_loop(0, 2, step, 0)

    beside(compute_for_across)

    def third(p, _):
        py = at(p)
        even = p % 2 == 0
        for q, ph in ((panel(x, z_far), h), (panel(1 - x, z_far), 1 - h)):
            arrived(q, py, ph)
            copy(q, py, ph, core_sem, sibling).start()

        @pl.when(p < 3)
        def _():
            for pz, sem, peer, on in ((z_down, up_sem, up, even), (z_up, down_sem, down, jnp.logical_not(even))):
                q = panel(x, pz)
                arrived(q, py, 1 - h)

                @pl.when(on)
                def _():
                    copy(q, py, 1 - h, sem, peer).start()
                copy(q, py, 1 - h, core_sem, sibling).start()
        return 0

    lax.fori_loop(0, 4, third, 0)
    compute_for_across(2, z_far)

    def near(i, _):
        whole(jnp.where(i == 0, x, 1 - x))
        return 0

    lax.fori_loop(0, 2, near, 0)
    beside(other_column)

    def fourth(p, _):
        py = at(p)
        q = panel(x, z_far)
        arrived(q, py, 1 - h)
        copy(q, py, 1 - h, core_sem, sibling).start()
        return 0

    lax.fori_loop(0, 3, fourth, 0)
    beside(same_column)
    other_column(2, z_far)
    same_column(2, z_far)

    for swap in swaps:
        swap.wait_send()

    for j in range(3):
        for i in range(3):
            lend(j, i).wait_send()

    def left(p, _):
        py = at(p)
        even = p % 2 == 0
        odd = jnp.logical_not(even)
        copy(mine, py, h, x_sem, across).wait_send()
        copy(other, py, 1 - h, x_sem, across).wait_send()
        for q, ph in ((mine, h), (other, 1 - h)):
            copy(q, py, ph, up_sem, up).wait_send()
            copy(q, py, ph, down_sem, down).wait_send()
        for ph in range(2):
            copy(mine, py, ph, core_sem, sibling).wait_send()
            copy(other, py, ph, core_sem, sibling).wait_send()
        for pz in (z_down, z_up, z_far):
            copy(panel(x, pz), py, h, core_sem, sibling).wait_send()
            copy(panel(1 - x, pz), py, 1 - h, core_sem, sibling).wait_send()

        @pl.when(p < 3)
        def _():
            copy(mine, py, 1 - h, up_sem, up).wait_send()
            copy(mine, py, 1 - h, down_sem, down).wait_send()
            for pz in (z_down, z_up, z_far):
                copy(panel(x, pz), py, 1 - h, core_sem, sibling).wait_send()

        for px, ph, on in ((x, h, True), (1 - x, 1 - h, True), (x, 1 - h, p < 3)):
            @pl.when(jnp.logical_and(even, on))
            def _():
                copy(panel(px, z_down), py, ph, up_sem, up).wait_send()

            @pl.when(jnp.logical_and(odd, on))
            def _():
                copy(panel(px, z_up), py, ph, down_sem, down).wait_send()
        return 0

    lax.fori_loop(0, 4, left, 0)


def group(rows):
    block = (N_LOOP, 4, 2)
    return pl.pallas_call(
        group_kernel,
        out_shape=pltpu.VMEM((PANEL, N_LOOP * PANEL), jnp.bfloat16),
        in_specs=[pl.BlockSpec(memory_space=pltpu.VMEM)],
        out_specs=pl.BlockSpec(memory_space=pltpu.VMEM),
        scratch_shapes=[
            pltpu.VMEM(block + (SHARE, FRAMES), jnp.bfloat16),
            pltpu.VMEM((3, 2, PANEL, PANEL // 2), jnp.bfloat16),
            pltpu.VMEM((3, 2, PANEL, PANEL // 2), jnp.bfloat16),
            pltpu.VMEM((3, PANEL, 128), jnp.bfloat16),
            pltpu.VMEM((3, PANEL, 128), jnp.bfloat16),
            pltpu.SemaphoreType.DMA((7,)),
            pltpu.SemaphoreType.DMA(block),
            pltpu.SemaphoreType.DMA(block),
            pltpu.SemaphoreType.DMA(block),
            pltpu.SemaphoreType.DMA(block),
            pltpu.SemaphoreType.DMA(block),
            pltpu.SemaphoreType.DMA((3, 3)),
            pltpu.SemaphoreType.DMA((3, 3)),
        ],
        compiler_params=pltpu.CompilerParams(
            collective_id=1, has_side_effects=True, vmem_limit_bytes=46 * 2**20
        ),
        name="group",
    )(rows)


def local(signal, width_class, kernel, taps, chosen):
    rows = front(signal, chosen.reshape(1, PANEL), width_class.reshape(CX * CY, CZ), kernel, taps)
    wide = group(rows.reshape(4, 2, SHARE, FRAMES))
    return wide.reshape(PANEL, 1, N_LOOP * PANEL)


def solution(mesh):
    in_specs = (
        P("slab", "loop", None, None),
        P("slab", "loop", None),
        P(),
        P(),
        P("loop", "slab", None),
    )
    return jax.shard_map(local, mesh=mesh, in_specs=in_specs, out_specs=P("loop", "slab", None), check_vma=False)
```

```python
import functools

import jax
import jax.numpy as jnp
from jax import lax
from jax.experimental import pallas as pl
from jax.experimental.pallas import tpu as pltpu
from jax.sharding import PartitionSpec as P

MESH = pl.DeviceIdType.MESH
CX, CY, CZ, FRAMES = 4, 4, 64, 1920
VOXELS = CX * CY * CZ
PANEL = 512
SHARE = 64
N_LOOP, N_SLAB = 16, 8
EDGES = (0, 384, 896, 1408, 1664, 1920)
CHUNKS = len(EDGES) - 1
WIDE = 384
REACH = 128
FILTER = 256
ORDER = (0, 1, 3, 2)


def front_kernel(sig, chosen, wclass, kernel, taps, rows, block, halo, vox, w_hi, w_lo, s_hi, s_lo, t_hi, t_lo, filt, sums, hop, load_sem, send_sem, recv_sem, first_sem, pass_sem, hop_sem, last_sem):
    loop, slab = lax.axis_index("loop"), lax.axis_index("slab")
    x, z, c = loop // 8, (loop // 2) % 4, loop % 2
    is_a, is_b = loop == 7, loop == 8
    has = (slab > 0, slab < N_SLAB - 1, jnp.logical_and(loop > 0, loop != 8), jnp.logical_and(loop < N_LOOP - 1, loop != 7))
    edge = (slab == 0, slab == N_SLAB - 1, loop == 0, loop == N_LOOP - 1)
    peers = ((loop, slab - 1), (loop, slab + 1), (loop - 1, slab), (loop + 1, slab))
    planes = (sig.at[0], sig.at[CX - 1], sig.at[:, 0], sig.at[:, CY - 1])
    lands = (1, 0, 3, 2)

    barrier = pltpu.get_barrier_semaphore()
    for there, peer in zip(has, peers):
        @pl.when(there)
        def _():
            pl.semaphore_signal(barrier, inc=1, device_id=peer, device_id_type=MESH)
    across = ((loop + 8) % N_LOOP, slab)
    pl.semaphore_signal(barrier, inc=1, device_id=across, device_id_type=MESH)
    for at_end, end in ((is_a, 7), (is_b, 8)):
        low = 0 if end == 7 else 9

        @pl.when(at_end)
        def _():
            for there in range(low, low + 7):
                pl.semaphore_signal(barrier, inc=1, device_id=(there, slab), device_id_type=MESH)

        @pl.when(jnp.logical_and(loop >= low, loop < low + 7))
        def _():
            pl.semaphore_signal(barrier, inc=1, device_id=(end, slab), device_id_type=MESH)
    load = pltpu.make_async_copy(sig, block, load_sem)
    load.start()
    ends = jnp.where(jnp.logical_or(is_a, is_b), 7, 1)
    pl.semaphore_wait(barrier, sum(there.astype(jnp.int32) for there in has) + 1 + ends)

    def leg(src, dst, send, recv, peer):
        return pltpu.make_async_remote_copy(
            src_ref=src, dst_ref=dst, send_sem=send, recv_sem=recv, device_id=(peer, slab), device_id_type=MESH
        )

    def first_legs():
        return (
            [leg(sig.at[j, CY - 1], hop, first_sem.at[j], hop_sem, 2 * j + 1 if j < 3 else 15) for j in range(4)],
            [leg(sig.at[j, 0], hop, first_sem.at[j], hop_sem, 8 + 2 * j if j > 0 else 0) for j in range(4)],
        )

    for at_end, legs in zip((is_a, is_b), first_legs()):
        @pl.when(at_end)
        def _():
            for one in legs:
                one.start()

    early_relay = jnp.logical_and(x + c == 1, jnp.logical_not(jnp.logical_or(is_a, is_b)))
    to_a = jnp.logical_and(x == 0, c == 0)
    to_b = jnp.logical_and(x == 1, c == 1)

    def hop_across():
        return leg(hop, hop, pass_sem, hop_sem, across[0])

    def hop_b():
        return leg(hop, halo.at[2, z], pass_sem, last_sem.at[z], 8)

    def hop_a():
        return leg(hop, halo.at[3, z], pass_sem, last_sem.at[z], 7)

    def halo_copy(d, k):
        lanes = pl.ds(EDGES[k], EDGES[k + 1] - EDGES[k])
        return pltpu.make_async_remote_copy(
            src_ref=planes[d].at[:, :, lanes],
            dst_ref=halo.at[lands[d], :, :, lanes],
            send_sem=send_sem.at[d, k],
            recv_sem=recv_sem.at[lands[d], k],
            device_id=peers[d],
            device_id_type=MESH,
        )

    def halo_wait(d, k):
        lanes = pl.ds(EDGES[k], EDGES[k + 1] - EDGES[k])
        pltpu.make_async_remote_copy(
            src_ref=halo.at[d, :, :, lanes],
            dst_ref=halo.at[d, :, :, lanes],
            send_sem=send_sem.at[d, k],
            recv_sem=recv_sem.at[d, k],
            device_id=peers[d],
            device_id_type=MESH,
        ).wait_recv()

    def send_chunks(chunks):
        for k in chunks:
            for d in range(4):
                @pl.when(has[d])
                def _():
                    halo_copy(d, k).start()

    send_chunks(range(2))

    for d in range(4):
        @pl.when(edge[d])
        def _():
            halo[d] = jnp.zeros_like(halo[d])
    for part in (s_hi, s_lo):
        part[:, 0:REACH] = jnp.zeros((PANEL, REACH), jnp.bfloat16)
        part[:, REACH + FRAMES :] = jnp.zeros((PANEL, REACH), jnp.bfloat16)

    def split(value):
        hi = value.astype(jnp.bfloat16)
        return hi, (value - hi.astype(jnp.float32)).astype(jnp.bfloat16)

    wide = FILTER + 2 * REACH
    lag = lax.broadcasted_iota(jnp.int32, (wide, FILTER), 0) - lax.broadcasted_iota(jnp.int32, (wide, FILTER), 1) - REACH + 4
    band = jnp.zeros((wide, FILTER), jnp.float32)
    for tap in range(9):
        band = jnp.where(lag == tap, taps[tap], band)
    t_hi[...], t_lo[...] = split(band)

    index = jnp.broadcast_to(chosen[...].astype(jnp.float32), (128, PANEL))
    vox[...] = jnp.transpose(index).astype(jnp.int32)
    tall = 64

    def build(t, _):
        at = pl.ds(pl.multiple_of(t * tall, tall), tall)
        v = vox[at, :]
        iota = lax.broadcasted_iota(jnp.int32, (tall, 128), 1)
        iota_z = lax.broadcasted_iota(jnp.int32, (tall, CZ), 1)
        hits = jnp.zeros((tall, CZ), jnp.int32)
        for run in range(CX * CY):
            hits = hits + jnp.where(v[:, :CZ] == iota_z + run * CZ, wclass[run : run + 1, :], 0)
        klass = jnp.sum(hits.astype(jnp.float32), axis=1, keepdims=True)
        weight = []
        for d in range(3):
            w = jnp.zeros_like(klass)
            for c in range(4):
                w = w + jnp.where(klass == float(c), kernel[d, c], 0.0)
            weight.append(jnp.broadcast_to(w, (tall, 128)))
        wx, wy, wz = weight
        centre = 1.0 - 2.0 * (wx + wy + wz)
        x, y, z = v >> 8, (v >> 6) & 3, v & 63
        none = jnp.full_like(v, -1)
        y_lo, y_hi = jnp.where(y > 0, v - CZ, none), jnp.where(y < CY - 1, v + CZ, none)
        z_lo, z_hi = jnp.where(z > 0, v - 1, none), jnp.where(z < CZ - 1, v + 1, none)
        plane = x * CZ + z

        def put(column, w):
            w_hi[at, column : column + 128], w_lo[at, column : column + 128] = split(w)

        zero = jnp.zeros((tall, 128), jnp.float32)
        for b in range(VOXELS // 128):
            col = iota + b * 128
            w = jnp.where(col == v, centre, zero)
            w = jnp.where((col == v - 256) | (col == v + 256), wx, w)
            w = jnp.where((col == y_lo) | (col == y_hi), wy, w)
            put(b * 128, jnp.where((col == z_lo) | (col == z_hi), wz, w))
        picks = (
            (v, wx),
            (v - 768, wx),
            (jnp.where(y == 0, plane, none), wy),
            (jnp.where(y == CY - 1, plane, none), wy),
        )
        for d, (pick, w) in enumerate(picks):
            for b in range(2):
                put(VOXELS + d * 256 + b * 128, jnp.where(iota + b * 128 == pick, w, zero))
        return 0

    lax.fori_loop(0, PANEL // tall, build, 0)

    @pl.when(early_relay)
    def _():
        hop_across().wait_recv()
        hop_across().start()

    send_chunks(range(2, CHUNKS))

    half = 256

    def product(ref, first, lanes, h):
        at = pl.ds(pl.multiple_of(h * half, half), half)
        right = ref[:, :, :, lanes].reshape(VOXELS, -1)
        cols = pl.ds(first, VOXELS)
        return jnp.dot(w_hi[at, cols], right, preferred_element_type=jnp.float32) + jnp.dot(
            w_lo[at, cols], right, preferred_element_type=jnp.float32
        )

    load.wait()

    def inner(i, _):
        k, h = i // 2, i % 2
        at = pl.ds(pl.multiple_of(h * half, half), half)
        lanes = pl.ds(pl.multiple_of(k * WIDE, 128), WIDE)
        filt[at, lanes] = product(block, 0, lanes, h)
        return 0

    lax.fori_loop(0, FRAMES // WIDE * 2, inner, 0)
    sums[...] = jnp.zeros_like(sums)

    for relay, onward in ((to_a, hop_a), (to_b, hop_b)):
        @pl.when(relay)
        def _():
            hop_across().wait_recv()
            onward().start()

    for at_end, onward in ((is_a, 3), (is_b, 2)):
        @pl.when(at_end)
        def _():
            for j in range(4):
                leg(hop, halo.at[onward, j], pass_sem, last_sem.at[j], 7).wait_recv()

    def filter_part(at, first, width):
        window = pl.ds(first, width + 2 * REACH)
        hi, lo = s_hi[at, window], s_lo[at, window]
        rows_of = pl.ds(0, width + 2 * REACH)
        cols = pl.ds(0, width)
        a, b = t_hi[rows_of, cols], t_lo[rows_of, cols]
        total = jnp.dot(hi, a, preferred_element_type=jnp.float32)
        total = total + jnp.dot(hi, b, preferred_element_type=jnp.float32)
        total = total + jnp.dot(lo, a, preferred_element_type=jnp.float32)
        filt[at, pl.ds(first, width)] = total
        for i in range(width // 128):
            sums[at, :] += total[:, i * 128 : (i + 1) * 128]

    for k in range(CHUNKS):
        for d in range(4):
            @pl.when(has[d])
            def _():
                halo_wait(d, k)

        lanes = pl.ds(EDGES[k], EDGES[k + 1] - EDGES[k])
        shifted = pl.ds(EDGES[k] + REACH, EDGES[k + 1] - EDGES[k])
        first = max(0, EDGES[k] - REACH)
        last = FRAMES if k == CHUNKS - 1 else EDGES[k + 1] - REACH

        def outer(h, _):
            at = pl.ds(pl.multiple_of(h * half, half), half)
            s_hi[at, shifted], s_lo[at, shifted] = split(filt[at, lanes] + product(halo, VOXELS, lanes, h))
            for start in range(first, last, FILTER):
                filter_part(at, start, min(FILTER, last - start))
            return 0

        lax.fori_loop(0, 2, outer, 0)

    deep = 64

    def norm(t, _):
        at = pl.ds(pl.multiple_of(t * deep, deep), deep)
        mean = jnp.sum(sums[at, :], axis=1, keepdims=True) * (1.0 / FRAMES)
        wide_mean = jnp.broadcast_to(mean, (deep, 128))
        square = jnp.zeros((deep, 128), jnp.float32)
        for i in range(FRAMES // 128):
            centred = filt[at, i * 128 : (i + 1) * 128] - wide_mean
            square = square + centred * centred
        scale = lax.rsqrt(jnp.sum(square, axis=1, keepdims=True) * (1.0 / FRAMES) + 1e-05)
        wide_scale = jnp.broadcast_to(scale, (deep, 128))
        for i in range(FRAMES // 128):
            lanes = slice(i * 128, (i + 1) * 128)
            rows[at, lanes] = ((filt[at, lanes] - wide_mean) * wide_scale).astype(jnp.bfloat16)
        return 0

    lax.fori_loop(0, PANEL // deep, norm, 0)

    for at_end, legs in zip((is_a, is_b), first_legs()):
        @pl.when(at_end)
        def _():
            for one in legs:
                one.wait_send()

    @pl.when(jnp.logical_not(jnp.logical_or(is_a, is_b)))
    def _():
        hop_across().wait_send()

    for k in range(CHUNKS):
        for d in range(4):
            @pl.when(has[d])
            def _():
                halo_copy(d, k).wait_send()


def front(signal, chosen, wclass, kernel, taps):
    vmem = pl.BlockSpec(memory_space=pltpu.VMEM)
    smem = pl.BlockSpec(memory_space=pltpu.SMEM)
    return pl.pallas_call(
        front_kernel,
        out_shape=pltpu.VMEM((PANEL, FRAMES), jnp.bfloat16),
        in_specs=[pl.BlockSpec(memory_space=pl.ANY), vmem, vmem, smem, smem],
        out_specs=vmem,
        scratch_shapes=[
            pltpu.VMEM((CX, CY, CZ, FRAMES), jnp.bfloat16),
            pltpu.VMEM((4, 4, CZ, FRAMES), jnp.bfloat16),
            pltpu.VMEM((PANEL, 128), jnp.int32),
            pltpu.VMEM((PANEL, 2 * VOXELS), jnp.bfloat16),
            pltpu.VMEM((PANEL, 2 * VOXELS), jnp.bfloat16),
            pltpu.VMEM((PANEL, FRAMES + 2 * REACH), jnp.bfloat16),
            pltpu.VMEM((PANEL, FRAMES + 2 * REACH), jnp.bfloat16),
            pltpu.VMEM((FILTER + 2 * REACH, FILTER), jnp.bfloat16),
            pltpu.VMEM((FILTER + 2 * REACH, FILTER), jnp.bfloat16),
            pltpu.VMEM((PANEL, FRAMES), jnp.float32),
            pltpu.VMEM((PANEL, 128), jnp.float32),
            pltpu.VMEM((CZ, FRAMES), jnp.bfloat16),
            pltpu.SemaphoreType.DMA,
            pltpu.SemaphoreType.DMA((4, CHUNKS)),
            pltpu.SemaphoreType.DMA((4, CHUNKS)),
            pltpu.SemaphoreType.DMA((4,)),
            pltpu.SemaphoreType.DMA,
            pltpu.SemaphoreType.DMA,
            pltpu.SemaphoreType.DMA((4,)),
        ],
        compiler_params=pltpu.CompilerParams(
            collective_id=0, has_side_effects=True, vmem_limit_bytes=56 * 2**20
        ),
        name="front",
    )(signal, chosen, wclass, kernel, taps)


def group_kernel(rows, tiles, held, x_out, x_in, z_out, z_in, swap_sem, x_sem, mate_sem, mirror_sem, core_sem, recv_sem, lend_sem, borrow_sem):
    loop, slab = lax.axis_index("loop"), lax.axis_index("slab")
    x, z, c = loop // 8, (loop // 2) % 4, loop % 2
    y, h = slab // 2, slab % 2
    z_mate, z_mirror, z_far = z + 1 - 2 * (z % 2), 3 - z, (z + 2) % 4

    def panel(px, pz, pc=None):
        return px * 8 + pz * 2 + (c if pc is None else pc)

    mate, mirror = (panel(x, z_mate), slab), (panel(x, z_mirror), slab)
    across, sibling = (panel(1 - x, z), slab), (panel(x, z, 1 - c), slab)
    inside = [(loop, ((y + dy) % 4) * 2 + h) for dy in (1, 3, 2)]
    outside = [(panel(1 - x, z), ((y + dy) % 4) * 2 + 1 - h) for dy in ORDER]

    barrier = pltpu.get_barrier_semaphore()
    peers = [mate, mirror, across, sibling] + inside + outside
    for peer in peers:
        pl.semaphore_signal(barrier, inc=1, device_id=peer, device_id_type=MESH)
    pl.semaphore_wait(barrier, len(peers))

    def at(p):
        dy = jnp.where(p == 2, 3, jnp.where(p == 3, 2, p))
        return (y + dy) % 4

    def copy(q, py, ph, sem, peer):
        return pltpu.make_async_remote_copy(
            src_ref=held.at[q, py, ph],
            dst_ref=held.at[q, py, ph],
            send_sem=sem.at[q, py, ph],
            recv_sem=recv_sem.at[q, py, ph],
            device_id=peer,
            device_id_type=MESH,
        )

    def arrived(q, py, ph):
        copy(q, py, ph, core_sem, sibling).wait_recv()

    swaps = []
    for i, peer in enumerate(outside + inside):
        to_y, to_h = peer[1] // 2, peer[1] % 2
        swaps.append(pltpu.make_async_remote_copy(
            src_ref=rows.at[to_y, to_h],
            dst_ref=held.at[loop, y, h],
            send_sem=swap_sem.at[i],
            recv_sem=recv_sem.at[loop, y, h],
            device_id=peer,
            device_id_type=MESH,
        ))
    pltpu.make_async_copy(rows.at[y, h], held.at[loop, y, h], recv_sem.at[loop, y, h]).start()
    for i in (0, 4, 1, 5, 2, 6, 3):
        swaps[i].start()

    mine, other = panel(x, z), panel(1 - x, z)

    def begin(p, _):
        py = at(p)

        @pl.when(p == 0)
        def _():
            pltpu.make_async_copy(rows.at[y, h], held.at[loop, y, h], recv_sem.at[loop, y, h]).wait()

        @pl.when(p > 0)
        def _():
            arrived(mine, py, h)
        copy(mine, py, h, mate_sem, mate).start()
        copy(mine, py, h, mirror_sem, mirror).start()
        copy(mine, py, h, x_sem, across).start()
        copy(mine, py, h, core_sem, sibling).start()
        arrived(other, py, 1 - h)
        copy(other, py, 1 - h, x_sem, across).start()
        copy(other, py, 1 - h, mate_sem, mate).start()
        copy(other, py, 1 - h, core_sem, sibling).start()
        return 0

    lax.fori_loop(0, 4, begin, 0)

    def onward(p, q, ph, odd):
        @pl.when(p % 2 == odd)
        def _():
            if odd:
                copy(q, at(p), ph, mate_sem, mate).start()
            else:
                copy(q, at(p), ph, mirror_sem, mirror).start()

    def second(p, _):
        py = at(p)
        arrived(mine, py, 1 - h)
        copy(mine, py, 1 - h, mirror_sem, mirror).start()
        copy(mine, py, 1 - h, mate_sem, mate).start()
        copy(mine, py, 1 - h, core_sem, sibling).start()
        for pz, odd in ((z_mirror, 1), (z_mate, 0)):
            q = panel(x, pz)
            arrived(q, py, h)
            onward(p, q, h, odd)
            copy(q, py, h, core_sem, sibling).start()
        for q, ph in ((panel(1 - x, z_mate), 1 - h), (other, h)):
            arrived(q, py, ph)
            copy(q, py, ph, core_sem, sibling).start()
        return 0

    lax.fori_loop(0, 4, second, 0)

    def from_sibling(px, pz, ph):
        def body(p, _):
            arrived(panel(px, pz, 1 - c), at(p), ph)
            return 0

        lax.fori_loop(0, 4, body, 0)

    def times(q, right):
        left = held[q].reshape(PANEL, FRAMES)
        product = lax.dot_general(left, right, (((1,), (1,)), ((), ())), preferred_element_type=jnp.float32)
        return product * (1.0 / FRAMES**0.5)

    def half(q, ph):
        return held[q, :, ph].reshape(PANEL // 2, FRAMES)

    def lend(axis, j, pc):
        out, into, peer = ((x_out, x_in, across), (z_out, z_in, mirror))[axis]
        return pltpu.make_async_remote_copy(
            src_ref=out.at[j, pc],
            dst_ref=into.at[j, pc],
            send_sem=lend_sem.at[axis, j, pc],
            recv_sem=borrow_sem.at[axis, j, pc],
            device_id=peer,
            device_id_type=MESH,
        )

    def lend_across(j, pz):
        from_sibling(x, pz, h)

        def body(pc, _):
            x_out[j, pc] = times(other, half(panel(x, pz, pc), h)).astype(jnp.bfloat16)
            lend(0, j, pc).start()
            return 0

        lax.fori_loop(0, 2, body, 0)

    def lend_mirror(j, pz):
        from_sibling(1 - x, pz, 1 - h)

        def body(pc, _):
            z_out[j, pc] = times(panel(x, z_mirror), half(panel(1 - x, pz, pc), 1 - h)).astype(jnp.bfloat16)
            lend(1, j, pc).start()
            return 0

        lax.fori_loop(0, 2, body, 0)

    def columns(q, first, width):
        return pl.ds(pl.multiple_of(q * PANEL + first, 128), width)

    def full(px, pz):
        def body(i, _):
            q, j = panel(px, pz, i // 2), i % 2
            right = held[q, pl.ds(2 * j, 2)].reshape(PANEL // 2, FRAMES)
            tiles[:, columns(q, j * 256, 256)] = times(loop, right).astype(jnp.bfloat16)
            return 0

        lax.fori_loop(0, 4, body, 0)

    lane = lax.broadcasted_iota(jnp.int32, (PANEL, 128), 1)

    def place(q, same, opposite):
        low, high = jnp.where(h == 0, same, opposite), jnp.where(h == 0, opposite, same)
        for i in range(2):
            a, b = low[:, i * 128 : (i + 1) * 128], high[:, i * 128 : (i + 1) * 128]
            first = jnp.where(lane < 64, a, pltpu.roll(b, 64, axis=1))
            after = jnp.where(lane < 64, pltpu.roll(a, 64, axis=1), b)
            tiles[:, columns(q, i * 256, 128)] = first.astype(jnp.bfloat16)
            tiles[:, columns(q, i * 256 + 128, 128)] = after.astype(jnp.bfloat16)

    def borrowed(axis, j, pc):
        lend(axis, j, pc).wait_recv()
        return (x_in, z_in)[axis][j, pc].astype(jnp.float32)

    def each_core(body):
        def step(pc, _):
            body(pc)
            return 0

        lax.fori_loop(0, 2, step, 0)

    def third(p, _):
        q = panel(x, z_mirror)
        arrived(q, at(p), 1 - h)
        onward(p, q, 1 - h, 1)
        copy(q, at(p), 1 - h, core_sem, sibling).start()
        return 0

    lax.fori_loop(0, 4, third, 0)

    def early(j, _):
        lend_mirror(j, jnp.where(j == 0, z, z_mate))
        lend_across(j, jnp.where(j == 0, z_mirror, z_mate))
        return 0

    lax.fori_loop(0, 2, early, 0)

    def fourth(p, _):
        py = at(p)
        q = panel(x, z_mate)
        arrived(q, py, 1 - h)
        onward(p, q, 1 - h, 0)
        copy(q, py, 1 - h, core_sem, sibling).start()
        q = panel(x, z_far)
        arrived(q, py, h)
        copy(q, py, h, core_sem, sibling).start()
        return 0

    lax.fori_loop(0, 4, fourth, 0)
    lend_across(2, z_far)

    from_sibling(x, z, 0)
    from_sibling(x, z, 1)
    from_sibling(1 - x, z, h)
    from_sibling(x, z_mirror, 1 - h)
    from_sibling(x, z_mate, 1 - h)

    def whole(i, _):
        full(jnp.where(i == 1, 1 - x, x), jnp.where(i == 2, z_mirror, jnp.where(i == 3, z_mate, z)))
        return 0

    lax.fori_loop(0, 4, whole, 0)

    def part_mate(pc):
        q = panel(1 - x, z_mate, pc)
        place(q, borrowed(0, 1, pc), times(loop, half(q, 1 - h)))

    def none_mirror(pc):
        place(panel(1 - x, z_mirror, pc), borrowed(0, 0, pc), borrowed(1, 0, pc))

    def none_far(pc):
        place(panel(1 - x, z_far, pc), borrowed(0, 2, pc), borrowed(1, 1, pc))

    each_core(part_mate)
    each_core(none_mirror)

    def fifth(p, _):
        q = panel(x, z_far)
        arrived(q, at(p), 1 - h)
        copy(q, at(p), 1 - h, core_sem, sibling).start()
        return 0

    lax.fori_loop(0, 4, fifth, 0)
    each_core(none_far)
    from_sibling(x, z_far, 1 - h)
    full(x, z_far)

    for swap in swaps:
        swap.wait_send()
    for axis, count in ((0, 3), (1, 2)):
        for j in range(count):
            for pc in range(2):
                lend(axis, j, pc).wait_send()

    def left(p, _):
        py = at(p)
        for q, ph in ((mine, h), (mine, 1 - h), (other, 1 - h)):
            copy(q, py, ph, mate_sem, mate).wait_send()
        for q, ph in ((mine, h), (mine, 1 - h)):
            copy(q, py, ph, mirror_sem, mirror).wait_send()
        for q, ph in ((mine, h), (other, 1 - h)):
            copy(q, py, ph, x_sem, across).wait_send()

        for ph in range(2):
            @pl.when(p % 2 == 1)
            def _():
                copy(panel(x, z_mirror), py, ph, mate_sem, mate).wait_send()

            @pl.when(p % 2 == 0)
            def _():
                copy(panel(x, z_mate), py, ph, mirror_sem, mirror).wait_send()
            for q in (mine, other, panel(x, z_mate), panel(x, z_mirror), panel(x, z_far)):
                copy(q, py, ph, core_sem, sibling).wait_send()
        copy(panel(1 - x, z_mate), py, 1 - h, core_sem, sibling).wait_send()
        return 0

    lax.fori_loop(0, 4, left, 0)


def group(rows):
    block = (N_LOOP, 4, 2)
    part = (2, PANEL, PANEL // 2)
    return pl.pallas_call(
        group_kernel,
        out_shape=pltpu.VMEM((PANEL, N_LOOP * PANEL), jnp.bfloat16),
        in_specs=[pl.BlockSpec(memory_space=pl.ANY)],
        out_specs=pl.BlockSpec(memory_space=pltpu.VMEM),
        scratch_shapes=[pltpu.VMEM(block + (SHARE, FRAMES), jnp.bfloat16)]
        + [pltpu.VMEM((count,) + part, jnp.bfloat16) for count in (3, 3, 2, 2)]
        + [pltpu.SemaphoreType.DMA((7,))]
        + [pltpu.SemaphoreType.DMA(block)] * 5
        + [pltpu.SemaphoreType.DMA((2, 3, 2))] * 2,
        compiler_params=pltpu.CompilerParams(
            collective_id=1, has_side_effects=True, vmem_limit_bytes=48 * 2**20
        ),
        name="group",
    )(pltpu.with_memory_space_constraint(rows, pltpu.VMEM))


def local(signal, width_class, kernel, taps, chosen):
    rows = front(signal, chosen.reshape(1, PANEL), width_class.reshape(CX * CY, CZ), kernel, taps)
    wide = group(rows.reshape(4, 2, SHARE, FRAMES))
    return wide.reshape(PANEL, 1, N_LOOP * PANEL)


def solution(mesh):
    in_specs = (
        P("slab", "loop", None, None),
        P("slab", "loop", None),
        P(),
        P(),
        P("loop", "slab", None),
    )
    return jax.shard_map(local, mesh=mesh, in_specs=in_specs, out_specs=P("loop", "slab", None), check_vma=False)
```

```python
import functools

import jax
import jax.numpy as jnp
from jax import lax
from jax.experimental import pallas as pl
from jax.experimental.pallas import tpu as pltpu
from jax.sharding import PartitionSpec as P

MESH = pl.DeviceIdType.MESH
CX, CY, CZ, FRAMES = 4, 4, 64, 1920
VOXELS = CX * CY * CZ
PANEL = 512
SHARE = 64
N_LOOP, N_SLAB = 16, 8
EDGES = (0, 384, 896, 1408, 1664, 1920)
CHUNKS = len(EDGES) - 1
WIDE = 384
REACH = 128
FILTER = 256
ORDER = (0, 1, 3, 2)


def front_kernel(sig, chosen, wclass, kernel, taps, rows, block, halo, vox, w_hi, w_lo, s_hi, s_lo, t_hi, t_lo, filt, sums, hop, load_sem, send_sem, recv_sem, first_sem, pass_sem, hop_sem, last_sem):
    loop, slab = lax.axis_index("loop"), lax.axis_index("slab")
    x, z, c = loop // 8, (loop // 2) % 4, loop % 2
    is_a, is_b = loop == 7, loop == 8
    has = (slab > 0, slab < N_SLAB - 1, jnp.logical_and(loop > 0, loop != 8), jnp.logical_and(loop < N_LOOP - 1, loop != 7))
    edge = (slab == 0, slab == N_SLAB - 1, loop == 0, loop == N_LOOP - 1)
    peers = ((loop, slab - 1), (loop, slab + 1), (loop - 1, slab), (loop + 1, slab))
    planes = (sig.at[0], sig.at[CX - 1], sig.at[:, 0], sig.at[:, CY - 1])
    lands = (1, 0, 3, 2)

    barrier = pltpu.get_barrier_semaphore()
    for there, peer in zip(has, peers):
        @pl.when(there)
        def _():
            pl.semaphore_signal(barrier, inc=1, device_id=peer, device_id_type=MESH)
    across = ((loop + 8) % N_LOOP, slab)
    pl.semaphore_signal(barrier, inc=1, device_id=across, device_id_type=MESH)
    for at_end, end in ((is_a, 7), (is_b, 8)):
        low = 0 if end == 7 else 9

        @pl.when(at_end)
        def _():
            for there in range(low, low + 7):
                pl.semaphore_signal(barrier, inc=1, device_id=(there, slab), device_id_type=MESH)

        @pl.when(jnp.logical_and(loop >= low, loop < low + 7))
        def _():
            pl.semaphore_signal(barrier, inc=1, device_id=(end, slab), device_id_type=MESH)
    load = pltpu.make_async_copy(sig, block, load_sem)
    load.start()
    ends = jnp.where(jnp.logical_or(is_a, is_b), 7, 1)
    pl.semaphore_wait(barrier, sum(there.astype(jnp.int32) for there in has) + 1 + ends)

    def leg(src, dst, send, recv, peer):
        return pltpu.make_async_remote_copy(
            src_ref=src, dst_ref=dst, send_sem=send, recv_sem=recv, device_id=(peer, slab), device_id_type=MESH
        )

    def first_legs():
        return (
            [leg(sig.at[j, CY - 1], hop, first_sem.at[j], hop_sem, 2 * j + 1 if j < 3 else 15) for j in range(4)],
            [leg(sig.at[j, 0], hop, first_sem.at[j], hop_sem, 8 + 2 * j if j > 0 else 0) for j in range(4)],
        )

    for at_end, legs in zip((is_a, is_b), first_legs()):
        @pl.when(at_end)
        def _():
            for one in legs:
                one.start()

    early_relay = jnp.logical_and(x + c == 1, jnp.logical_not(jnp.logical_or(is_a, is_b)))
    to_a = jnp.logical_and(x == 0, c == 0)
    to_b = jnp.logical_and(x == 1, c == 1)

    def hop_across():
        return leg(hop, hop, pass_sem, hop_sem, across[0])

    def hop_b():
        return leg(hop, halo.at[2, z], pass_sem, last_sem.at[z], 8)

    def hop_a():
        return leg(hop, halo.at[3, z], pass_sem, last_sem.at[z], 7)

    def halo_copy(d, k):
        lanes = pl.ds(EDGES[k], EDGES[k + 1] - EDGES[k])
        return pltpu.make_async_remote_copy(
            src_ref=planes[d].at[:, :, lanes],
            dst_ref=halo.at[lands[d], :, :, lanes],
            send_sem=send_sem.at[d, k],
            recv_sem=recv_sem.at[lands[d], k],
            device_id=peers[d],
            device_id_type=MESH,
        )

    def halo_wait(d, k):
        lanes = pl.ds(EDGES[k], EDGES[k + 1] - EDGES[k])
        pltpu.make_async_remote_copy(
            src_ref=halo.at[d, :, :, lanes],
            dst_ref=halo.at[d, :, :, lanes],
            send_sem=send_sem.at[d, k],
            recv_sem=recv_sem.at[d, k],
            device_id=peers[d],
            device_id_type=MESH,
        ).wait_recv()

    def send_chunks(chunks):
        for k in chunks:
            for d in range(4):
                @pl.when(has[d])
                def _():
                    halo_copy(d, k).start()

    send_chunks(range(2))

    for d in range(4):
        @pl.when(edge[d])
        def _():
            halo[d] = jnp.zeros_like(halo[d])
    for part in (s_hi, s_lo):
        part[:, 0:REACH] = jnp.zeros((PANEL, REACH), jnp.bfloat16)
        part[:, REACH + FRAMES :] = jnp.zeros((PANEL, REACH), jnp.bfloat16)

    def split(value):
        hi = value.astype(jnp.bfloat16)
        return hi, (value - hi.astype(jnp.float32)).astype(jnp.bfloat16)

    wide = FILTER + 2 * REACH
    lag = lax.broadcasted_iota(jnp.int32, (wide, FILTER), 0) - lax.broadcasted_iota(jnp.int32, (wide, FILTER), 1) - REACH + 4
    band = jnp.zeros((wide, FILTER), jnp.float32)
    for tap in range(9):
        band = jnp.where(lag == tap, taps[tap], band)
    t_hi[...], t_lo[...] = split(band)

    index = jnp.broadcast_to(chosen[...].astype(jnp.float32), (128, PANEL))
    vox[...] = jnp.transpose(index).astype(jnp.int32)
    tall = 64

    def build(t, _):
        at = pl.ds(pl.multiple_of(t * tall, tall), tall)
        v = vox[at, :]
        iota = lax.broadcasted_iota(jnp.int32, (tall, 128), 1)
        iota_z = lax.broadcasted_iota(jnp.int32, (tall, CZ), 1)
        hits = jnp.zeros((tall, CZ), jnp.int32)
        for run in range(CX * CY):
            hits = hits + jnp.where(v[:, :CZ] == iota_z + run * CZ, wclass[run : run + 1, :], 0)
        klass = jnp.sum(hits.astype(jnp.float32), axis=1, keepdims=True)
        weight = []
        for d in range(3):
            w = jnp.zeros_like(klass)
            for c in range(4):
                w = w + jnp.where(klass == float(c), kernel[d, c], 0.0)
            weight.append(jnp.broadcast_to(w, (tall, 128)))
        wx, wy, wz = weight
        centre = 1.0 - 2.0 * (wx + wy + wz)
        x, y, z = v >> 8, (v >> 6) & 3, v & 63
        none = jnp.full_like(v, -1)
        y_lo, y_hi = jnp.where(y > 0, v - CZ, none), jnp.where(y < CY - 1, v + CZ, none)
        z_lo, z_hi = jnp.where(z > 0, v - 1, none), jnp.where(z < CZ - 1, v + 1, none)
        plane = x * CZ + z

        def put(column, w):
            w_hi[at, column : column + 128], w_lo[at, column : column + 128] = split(w)

        zero = jnp.zeros((tall, 128), jnp.float32)
        for b in range(VOXELS // 128):
            col = iota + b * 128
            w = jnp.where(col == v, centre, zero)
            w = jnp.where((col == v - 256) | (col == v + 256), wx, w)
            w = jnp.where((col == y_lo) | (col == y_hi), wy, w)
            put(b * 128, jnp.where((col == z_lo) | (col == z_hi), wz, w))
        picks = (
            (v, wx),
            (v - 768, wx),
            (jnp.where(y == 0, plane, none), wy),
            (jnp.where(y == CY - 1, plane, none), wy),
        )
        for d, (pick, w) in enumerate(picks):
            for b in range(2):
                put(VOXELS + d * 256 + b * 128, jnp.where(iota + b * 128 == pick, w, zero))
        return 0

    lax.fori_loop(0, PANEL // tall, build, 0)

    @pl.when(early_relay)
    def _():
        hop_across().wait_recv()
        hop_across().start()

    send_chunks(range(2, CHUNKS))

    half = 256

    def product(ref, first, lanes, h):
        at = pl.ds(pl.multiple_of(h * half, half), half)
        right = ref[:, :, :, lanes].reshape(VOXELS, -1)
        cols = pl.ds(first, VOXELS)
        return jnp.dot(w_hi[at, cols], right, preferred_element_type=jnp.float32) + jnp.dot(
            w_lo[at, cols], right, preferred_element_type=jnp.float32
        )

    load.wait()

    def inner(i, _):
        k, h = i // 2, i % 2
        at = pl.ds(pl.multiple_of(h * half, half), half)
        lanes = pl.ds(pl.multiple_of(k * WIDE, 128), WIDE)
        filt[at, lanes] = product(block, 0, lanes, h)
        return 0

    lax.fori_loop(0, FRAMES // WIDE * 2, inner, 0)
    sums[...] = jnp.zeros_like(sums)

    for relay, onward in ((to_a, hop_a), (to_b, hop_b)):
        @pl.when(relay)
        def _():
            hop_across().wait_recv()
            onward().start()

    for at_end, onward in ((is_a, 3), (is_b, 2)):
        @pl.when(at_end)
        def _():
            for j in range(4):
                leg(hop, halo.at[onward, j], pass_sem, last_sem.at[j], 7).wait_recv()

    def filter_part(at, first, width):
        window = pl.ds(first, width + 2 * REACH)
        hi, lo = s_hi[at, window], s_lo[at, window]
        rows_of = pl.ds(0, width + 2 * REACH)
        cols = pl.ds(0, width)
        a, b = t_hi[rows_of, cols], t_lo[rows_of, cols]
        total = jnp.dot(hi, a, preferred_element_type=jnp.float32)
        total = total + jnp.dot(hi, b, preferred_element_type=jnp.float32)
        total = total + jnp.dot(lo, a, preferred_element_type=jnp.float32)
        filt[at, pl.ds(first, width)] = total
        for i in range(width // 128):
            sums[at, :] += total[:, i * 128 : (i + 1) * 128]

    for k in range(CHUNKS):
        for d in range(4):
            @pl.when(has[d])
            def _():
                halo_wait(d, k)

        lanes = pl.ds(EDGES[k], EDGES[k + 1] - EDGES[k])
        shifted = pl.ds(EDGES[k] + REACH, EDGES[k + 1] - EDGES[k])
        first = max(0, EDGES[k] - REACH)
        last = FRAMES if k == CHUNKS - 1 else EDGES[k + 1] - REACH

        def outer(h, _):
            at = pl.ds(pl.multiple_of(h * half, half), half)
            s_hi[at, shifted], s_lo[at, shifted] = split(filt[at, lanes] + product(halo, VOXELS, lanes, h))
            for start in range(first, last, FILTER):
                filter_part(at, start, min(FILTER, last - start))
            return 0

        lax.fori_loop(0, 2, outer, 0)

    deep = 64

    def norm(t, _):
        at = pl.ds(pl.multiple_of(t * deep, deep), deep)
        mean = jnp.sum(sums[at, :], axis=1, keepdims=True) * (1.0 / FRAMES)
        wide_mean = jnp.broadcast_to(mean, (deep, 128))
        square = jnp.zeros((deep, 128), jnp.float32)
        for i in range(FRAMES // 128):
            centred = filt[at, i * 128 : (i + 1) * 128] - wide_mean
            square = square + centred * centred
        scale = lax.rsqrt(jnp.sum(square, axis=1, keepdims=True) * (1.0 / FRAMES) + 1e-05)
        wide_scale = jnp.broadcast_to(scale, (deep, 128))
        for i in range(FRAMES // 128):
            lanes = slice(i * 128, (i + 1) * 128)
            rows[at, lanes] = ((filt[at, lanes] - wide_mean) * wide_scale).astype(jnp.bfloat16)
        return 0

    lax.fori_loop(0, PANEL // deep, norm, 0)

    for at_end, legs in zip((is_a, is_b), first_legs()):
        @pl.when(at_end)
        def _():
            for one in legs:
                one.wait_send()

    @pl.when(jnp.logical_not(jnp.logical_or(is_a, is_b)))
    def _():
        hop_across().wait_send()

    for k in range(CHUNKS):
        for d in range(4):
            @pl.when(has[d])
            def _():
                halo_copy(d, k).wait_send()


def front(signal, chosen, wclass, kernel, taps):
    vmem = pl.BlockSpec(memory_space=pltpu.VMEM)
    smem = pl.BlockSpec(memory_space=pltpu.SMEM)
    return pl.pallas_call(
        front_kernel,
        out_shape=pltpu.VMEM((PANEL, FRAMES), jnp.bfloat16),
        in_specs=[pl.BlockSpec(memory_space=pl.ANY), vmem, vmem, smem, smem],
        out_specs=vmem,
        scratch_shapes=[
            pltpu.VMEM((CX, CY, CZ, FRAMES), jnp.bfloat16),
            pltpu.VMEM((4, 4, CZ, FRAMES), jnp.bfloat16),
            pltpu.VMEM((PANEL, 128), jnp.int32),
            pltpu.VMEM((PANEL, 2 * VOXELS), jnp.bfloat16),
            pltpu.VMEM((PANEL, 2 * VOXELS), jnp.bfloat16),
            pltpu.VMEM((PANEL, FRAMES + 2 * REACH), jnp.bfloat16),
            pltpu.VMEM((PANEL, FRAMES + 2 * REACH), jnp.bfloat16),
            pltpu.VMEM((FILTER + 2 * REACH, FILTER), jnp.bfloat16),
            pltpu.VMEM((FILTER + 2 * REACH, FILTER), jnp.bfloat16),
            pltpu.VMEM((PANEL, FRAMES), jnp.float32),
            pltpu.VMEM((PANEL, 128), jnp.float32),
            pltpu.VMEM((CZ, FRAMES), jnp.bfloat16),
            pltpu.SemaphoreType.DMA,
            pltpu.SemaphoreType.DMA((4, CHUNKS)),
            pltpu.SemaphoreType.DMA((4, CHUNKS)),
            pltpu.SemaphoreType.DMA((4,)),
            pltpu.SemaphoreType.DMA,
            pltpu.SemaphoreType.DMA,
            pltpu.SemaphoreType.DMA((4,)),
        ],
        compiler_params=pltpu.CompilerParams(
            collective_id=0, has_side_effects=True, vmem_limit_bytes=56 * 2**20
        ),
        name="front",
    )(signal, chosen, wclass, kernel, taps)


def correlate(left, right):
    product = lax.dot_general(
        left.reshape(PANEL, FRAMES), right, (((1,), (1,)), ((), ())), preferred_element_type=jnp.float32
    )
    return product * (1.0 / FRAMES**0.5)


def interleave(h, same, opposite):
    low, high = jnp.where(h == 0, same, opposite), jnp.where(h == 0, opposite, same)
    lane = lax.broadcasted_iota(jnp.int32, (PANEL, 128), 1)
    parts = []
    for i in range(2):
        a, b = low[:, i * 128 : (i + 1) * 128], high[:, i * 128 : (i + 1) * 128]
        parts.append(jnp.where(lane < 64, a, pltpu.roll(b, 64, axis=1)).astype(jnp.bfloat16))
        parts.append(jnp.where(lane < 64, pltpu.roll(a, 64, axis=1), b).astype(jnp.bfloat16))
    return parts


def group_kernel(rows, tiles, own, far_rest, far_part, held, x_out, x_in, z_out, z_in, swap_sem, x_sem, mate_sem, mirror_sem, core_sem, recv_sem, lend_sem, borrow_sem, own_sem):
    loop, slab = lax.axis_index("loop"), lax.axis_index("slab")
    x, z, c = loop // 8, (loop // 2) % 4, loop % 2
    y, h = slab // 2, slab % 2
    z_mate, z_mirror, z_far = z + 1 - 2 * (z % 2), 3 - z, (z + 2) % 4

    def panel(px, pz, pc=None):
        return px * 8 + pz * 2 + (c if pc is None else pc)

    mate, mirror = (panel(x, z_mate), slab), (panel(x, z_mirror), slab)
    across, sibling = (panel(1 - x, z), slab), (panel(x, z, 1 - c), slab)
    inside = [(loop, ((y + dy) % 4) * 2 + h) for dy in (1, 3, 2)]
    outside = [(panel(1 - x, z), ((y + dy) % 4) * 2 + 1 - h) for dy in ORDER]

    barrier = pltpu.get_barrier_semaphore()
    peers = [mate, mirror, across, sibling] + inside + outside
    for peer in peers:
        pl.semaphore_signal(barrier, inc=1, device_id=peer, device_id_type=MESH)
    pl.semaphore_wait(barrier, len(peers))

    def at(p):
        dy = jnp.where(p == 2, 3, jnp.where(p == 3, 2, p))
        return (y + dy) % 4

    def copy(q, py, ph, sem, peer):
        return pltpu.make_async_remote_copy(
            src_ref=held.at[q, py, ph],
            dst_ref=held.at[q, py, ph],
            send_sem=sem.at[q, py, ph],
            recv_sem=recv_sem.at[q, py, ph],
            device_id=peer,
            device_id_type=MESH,
        )

    def copy_far(q, py, sem, peer, src):
        return pltpu.make_async_remote_copy(
            src_ref=src,
            dst_ref=far_rest.at[c, py],
            send_sem=sem.at[q, py, 1 - h],
            recv_sem=recv_sem.at[q, py, 1 - h],
            device_id=peer,
            device_id_type=MESH,
        )

    def arrived(q, py, ph):
        copy(q, py, ph, core_sem, sibling).wait_recv()

    swaps = []
    for i, peer in enumerate(outside + inside):
        to_y, to_h = peer[1] // 2, peer[1] % 2
        swaps.append(pltpu.make_async_remote_copy(
            src_ref=rows.at[to_y, to_h],
            dst_ref=held.at[loop, y, h],
            send_sem=swap_sem.at[i],
            recv_sem=recv_sem.at[loop, y, h],
            device_id=peer,
            device_id_type=MESH,
        ))
    pltpu.make_async_copy(rows.at[y, h], held.at[loop, y, h], recv_sem.at[loop, y, h]).start()
    for i in (0, 4, 1, 5, 2, 6, 3):
        swaps[i].start()

    mine, other = panel(x, z), panel(1 - x, z)

    def own_rest(p):
        py = at(p)
        arrived(mine, py, 1 - h)
        copy(mine, py, 1 - h, mirror_sem, mirror).start()
        copy(mine, py, 1 - h, core_sem, sibling).start()

    def begin(p, _):
        py = at(p)

        @pl.when(p == 0)
        def _():
            pltpu.make_async_copy(rows.at[y, h], held.at[loop, y, h], recv_sem.at[loop, y, h]).wait()
            copy(mine, py, h, x_sem, across).start()

        @pl.when(p > 0)
        def _():
            arrived(mine, py, h)
        copy(mine, py, h, mirror_sem, mirror).start()
        copy(mine, py, h, mate_sem, mate).start()
        copy(mine, py, h, core_sem, sibling).start()

        @pl.when(p >= 2)
        def _():
            own_rest(p - 2)
        arrived(other, py, 1 - h)
        copy(other, py, 1 - h, x_sem, across).start()
        copy(other, py, 1 - h, mate_sem, mate).start()
        copy(other, py, 1 - h, core_sem, sibling).start()

        @pl.when(p == 2)
        def _():
            copy(mine, at(1), h, x_sem, across).start()
        return 0

    lax.fori_loop(0, 4, begin, 0)
    copy(mine, at(2), h, x_sem, across).start()
    copy(mine, at(3), h, x_sem, across).start()

    def onward(p, q, odd, rest):
        sem, peer = (mate_sem, mate) if odd else (mirror_sem, mirror)

        @pl.when(p % 2 == odd)
        def _():
            if rest:
                copy_far(q, at(p), sem, peer, held.at[q, at(p), 1 - h]).start()
            else:
                copy(q, at(p), h, sem, peer).start()

    def second(p, _):
        py = at(p)
        for pz, odd in ((z_mirror, 1), (z_mate, 0)):
            q = panel(x, pz)
            arrived(q, py, h)
            onward(p, q, odd, False)
            copy(q, py, h, core_sem, sibling).start()
        q = panel(1 - x, z_mate)
        arrived(q, py, 1 - h)
        copy(q, py, 1 - h, core_sem, sibling).start()
        return 0

    own_rest(2)
    lax.fori_loop(0, 4, second, 0)
    own_rest(3)

    def rest_to_mate(p, _):
        copy(mine, at(p), 1 - h, mate_sem, mate).start()
        return 0

    lax.fori_loop(0, 4, rest_to_mate, 0)

    def came_across(p, _):
        arrived(other, at(p), h)
        copy(other, at(p), h, core_sem, sibling).start()
        return 0

    lax.fori_loop(0, 4, came_across, 0)

    def from_sibling(px, pz, ph):
        def body(p, _):
            arrived(panel(px, pz, 1 - c), at(p), ph)
            return 0

        lax.fori_loop(0, 4, body, 0)

    def times(q, right):
        return correlate(held[q], right)

    def half(q, ph):
        return held[q, :, ph].reshape(PANEL // 2, FRAMES)

    def lend(axis, j, pc):
        out, into, peer = ((x_out, x_in, across), (z_out, z_in, mirror))[axis]
        return pltpu.make_async_remote_copy(
            src_ref=out.at[j, pc],
            dst_ref=into.at[j, pc],
            send_sem=lend_sem.at[axis, j, pc],
            recv_sem=borrow_sem.at[axis, j, pc],
            device_id=peer,
            device_id_type=MESH,
        )

    def lend_across(j, pz):
        from_sibling(x, pz, h)

        def body(pc, _):
            x_out[j, pc] = times(other, half(panel(x, pz, pc), h)).astype(jnp.bfloat16)
            lend(0, j, pc).start()
            return 0

        lax.fori_loop(0, 2, body, 0)

    def lend_mirror(j, pz):
        from_sibling(1 - x, pz, 1 - h)

        def body(pc, _):
            z_out[j, pc] = times(panel(x, z_mirror), half(panel(1 - x, pz, pc), 1 - h)).astype(jnp.bfloat16)
            lend(1, j, pc).start()
            return 0

        lax.fori_loop(0, 2, body, 0)

    def columns(q, first, width):
        return pl.ds(pl.multiple_of(q * PANEL + first, 128), width)

    def full(px, pz):
        def body(i, _):
            q, j = panel(px, pz, i // 2), i % 2
            right = held[q, pl.ds(2 * j, 2)].reshape(PANEL // 2, FRAMES)
            tiles[:, columns(q, j * 256, 256)] = times(loop, right).astype(jnp.bfloat16)
            return 0

        lax.fori_loop(0, 4, body, 0)

    def place(q, same, opposite):
        for i, part in enumerate(interleave(h, same, opposite)):
            tiles[:, columns(q, i * 128, 128)] = part

    def borrowed(axis, j, pc):
        lend(axis, j, pc).wait_recv()
        return (x_in, z_in)[axis][j, pc].astype(jnp.float32)

    def each_core(body):
        def step(pc, _):
            body(pc)
            return 0

        lax.fori_loop(0, 2, step, 0)

    def early_across(j, _):
        lend_across(j, jnp.where(j == 0, z_mirror, z_mate))
        return 0

    lax.fori_loop(0, 2, early_across, 0)

    def third(p, _):
        q = panel(x, z_mirror)
        arrived(q, at(p), 1 - h)
        onward(p, q, 1, True)
        copy(q, at(p), 1 - h, core_sem, sibling).start()
        return 0

    lax.fori_loop(0, 4, third, 0)

    def to_mirror(j, _):
        lend_mirror(j, jnp.where(j == 0, z, z_mate))
        return 0

    lax.fori_loop(0, 2, to_mirror, 0)

    keep = pltpu.make_async_copy(held.at[loop], own, own_sem)
    keep.start()
    from_sibling(x, z, 0)
    from_sibling(x, z, 1)
    full(x, z)

    def from_far(p, _):
        q = panel(x, z_far)
        arrived(q, at(p), h)
        copy(q, at(p), h, core_sem, sibling).start()
        return 0

    lax.fori_loop(0, 4, from_far, 0)
    lend_across(2, z_far)
    from_sibling(1 - x, z, h)
    full(1 - x, z)

    def fourth(p, _):
        q = panel(x, z_mate)
        arrived(q, at(p), 1 - h)
        onward(p, q, 0, True)
        copy(q, at(p), 1 - h, core_sem, sibling).start()
        return 0

    lax.fori_loop(0, 4, fourth, 0)

    from_sibling(x, z_mirror, 1 - h)
    from_sibling(x, z_mate, 1 - h)

    def whole(i, _):
        full(x, jnp.where(i == 0, z_mirror, z_mate))
        return 0

    lax.fori_loop(0, 2, whole, 0)

    def part_mate(pc):
        q = panel(1 - x, z_mate, pc)
        place(q, borrowed(0, 1, pc), times(loop, half(q, 1 - h)))

    def none_mirror(pc):
        place(panel(1 - x, z_mirror, pc), borrowed(0, 0, pc), borrowed(1, 0, pc))

    def none_far(pc):
        place(panel(1 - x, z_far, pc), borrowed(0, 2, pc), borrowed(1, 1, pc))

    def first_far(pc):
        far_part[pc] = times(loop, half(panel(x, z_far, pc), h)).astype(jnp.bfloat16)

    each_core(part_mate)
    each_core(first_far)
    each_core(none_mirror)

    def fifth(p, _):
        q = panel(x, z_far)
        arrived(q, at(p), 1 - h)
        copy_far(q, at(p), core_sem, sibling, far_rest.at[c, at(p)]).start()
        return 0

    lax.fori_loop(0, 4, fifth, 0)
    each_core(none_far)

    from_sibling(x, z_far, 1 - h)

    keep.wait()
    for swap in swaps:
        swap.wait_send()
    for axis, count in ((0, 3), (1, 2)):
        for j in range(count):
            for pc in range(2):
                lend(axis, j, pc).wait_send()

    def left(p, _):
        py = at(p)
        for q, ph in ((mine, h), (mine, 1 - h), (other, 1 - h)):
            copy(q, py, ph, mate_sem, mate).wait_send()
        for q, ph in ((mine, h), (mine, 1 - h)):
            copy(q, py, ph, mirror_sem, mirror).wait_send()
        for q, ph in ((mine, h), (other, 1 - h)):
            copy(q, py, ph, x_sem, across).wait_send()

        for ph in range(2):
            @pl.when(p % 2 == 1)
            def _():
                copy(panel(x, z_mirror), py, ph, mate_sem, mate).wait_send()

            @pl.when(p % 2 == 0)
            def _():
                copy(panel(x, z_mate), py, ph, mirror_sem, mirror).wait_send()
            for q in (mine, other, panel(x, z_mate), panel(x, z_mirror)):
                copy(q, py, ph, core_sem, sibling).wait_send()
        copy(panel(x, z_far), py, h, core_sem, sibling).wait_send()
        copy_far(panel(x, z_far), py, core_sem, sibling, far_rest.at[c, py]).wait_send()
        copy(panel(1 - x, z_mate), py, 1 - h, core_sem, sibling).wait_send()
        return 0

    lax.fori_loop(0, 4, left, 0)


def group(rows):
    block = (N_LOOP, 4, 2)
    part = (2, PANEL, PANEL // 2)
    return pl.pallas_call(
        group_kernel,
        out_shape=(
            pltpu.VMEM((PANEL, N_LOOP * PANEL), jnp.bfloat16),
            pltpu.VMEM((4, 2, SHARE, FRAMES), jnp.bfloat16),
            pltpu.VMEM((2, 4, SHARE, FRAMES), jnp.bfloat16),
            pltpu.VMEM(part, jnp.bfloat16),
        ),
        in_specs=[pl.BlockSpec(memory_space=pl.ANY)],
        out_specs=(pl.BlockSpec(memory_space=pltpu.VMEM),) * 4,
        scratch_shapes=[pltpu.VMEM(block + (SHARE, FRAMES), jnp.bfloat16)]
        + [pltpu.VMEM((count,) + part, jnp.bfloat16) for count in (3, 3, 2, 2)]
        + [pltpu.SemaphoreType.DMA((7,))]
        + [pltpu.SemaphoreType.DMA(block)] * 5
        + [pltpu.SemaphoreType.DMA((2, 3, 2))] * 2
        + [pltpu.SemaphoreType.DMA],
        compiler_params=pltpu.CompilerParams(
            collective_id=1, has_side_effects=True, vmem_limit_bytes=40 * 2**20
        ),
        name="group",
    )(pltpu.with_memory_space_constraint(rows, pltpu.VMEM))


def finish_kernel(tiles, own, far_rest, far_part, out, stage, sems):
    loop, h = lax.axis_index("loop"), lax.axis_index("slab") % 2
    far = loop // 8 * 4 + (loop // 2 + 2) % 4
    wide = 2 * PANEL

    def columns(pair):
        return pl.ds(pl.multiple_of(pair * wide, wide), wide)

    def ready(i):
        pair = (far + 1 + i) % 8
        return pltpu.make_async_copy(tiles.at[:, columns(pair)], out.at[:, columns(pair)], sems.at[i])

    for i in range(7):
        ready(i).start()

    def body(pc, _):
        right = far_rest[pc].reshape(PANEL // 2, FRAMES)
        parts = interleave(h, far_part[pc].astype(jnp.float32), correlate(own[...], right))
        for i, part in enumerate(parts):
            stage[:, pl.ds(pl.multiple_of(pc * PANEL + i * 128, 128), 128)] = part
        return 0

    lax.fori_loop(0, 2, body, 0)
    last = pltpu.make_async_copy(stage, out.at[:, columns(far)], sems.at[7])
    last.start()
    for i in range(7):
        ready(i).wait()
    last.wait()


def finish(tiles, own, far_rest, far_part):
    return pl.pallas_call(
        finish_kernel,
        out_shape=jax.ShapeDtypeStruct((PANEL, N_LOOP * PANEL), jnp.bfloat16),
        in_specs=[pl.BlockSpec(memory_space=pl.ANY)] + [pl.BlockSpec(memory_space=pltpu.VMEM)] * 3,
        out_specs=pl.BlockSpec(memory_space=pl.ANY),
        scratch_shapes=[pltpu.VMEM((PANEL, 2 * PANEL), jnp.bfloat16), pltpu.SemaphoreType.DMA((8,))],
        compiler_params=pltpu.CompilerParams(vmem_limit_bytes=12 * 2**20),
        name="finish",
    )(*(pltpu.with_memory_space_constraint(array, pltpu.VMEM) for array in (tiles, own, far_rest, far_part)))


def local(signal, width_class, kernel, taps, chosen):
    rows = front(signal, chosen.reshape(1, PANEL), width_class.reshape(CX * CY, CZ), kernel, taps)
    wide = finish(*group(rows.reshape(4, 2, SHARE, FRAMES)))
    return wide.reshape(PANEL, 1, N_LOOP * PANEL)


def solution(mesh):
    in_specs = (
        P("slab", "loop", None, None),
        P("slab", "loop", None),
        P(),
        P(),
        P("loop", "slab", None),
    )
    return jax.shard_map(local, mesh=mesh, in_specs=in_specs, out_specs=P("loop", "slab", None), check_vma=False)
```

```python
import functools

import jax
import jax.numpy as jnp
from jax import lax
from jax.experimental import pallas as pl
from jax.experimental.pallas import tpu as pltpu
from jax.sharding import PartitionSpec as P

MESH = pl.DeviceIdType.MESH
CX, CY, CZ, FRAMES = 4, 4, 64, 1920
VOXELS = CX * CY * CZ
PANEL = 512
SHARE = 64
N_LOOP, N_SLAB = 16, 8
EDGES = (0, 384, 896, 1408, 1664, 1920)
CHUNKS = len(EDGES) - 1
WIDE = 384
REACH = 128
FILTER = 256
ORDER = (0, 1, 3, 2)


def front_kernel(sig, chosen, wclass, kernel, taps, rows, block, halo, vox, w_hi, w_lo, s_hi, s_lo, t_hi, t_lo, filt, sums, hop, load_sem, send_sem, recv_sem, first_sem, pass_sem, hop_sem, last_sem):
    loop, slab = lax.axis_index("loop"), lax.axis_index("slab")
    x, z, c = loop // 8, (loop // 2) % 4, loop % 2
    is_a, is_b = loop == 7, loop == 8
    has = (slab > 0, slab < N_SLAB - 1, jnp.logical_and(loop > 0, loop != 8), jnp.logical_and(loop < N_LOOP - 1, loop != 7))
    edge = (slab == 0, slab == N_SLAB - 1, loop == 0, loop == N_LOOP - 1)
    peers = ((loop, slab - 1), (loop, slab + 1), (loop - 1, slab), (loop + 1, slab))
    planes = (sig.at[0], sig.at[CX - 1], sig.at[:, 0], sig.at[:, CY - 1])
    lands = (1, 0, 3, 2)

    barrier = pltpu.get_barrier_semaphore()
    for there, peer in zip(has, peers):
        @pl.when(there)
        def _():
            pl.semaphore_signal(barrier, inc=1, device_id=peer, device_id_type=MESH)
    across = ((loop + 8) % N_LOOP, slab)
    pl.semaphore_signal(barrier, inc=1, device_id=across, device_id_type=MESH)
    for at_end, end in ((is_a, 7), (is_b, 8)):
        low = 0 if end == 7 else 9

        @pl.when(at_end)
        def _():
            for there in range(low, low + 7):
                pl.semaphore_signal(barrier, inc=1, device_id=(there, slab), device_id_type=MESH)

        @pl.when(jnp.logical_and(loop >= low, loop < low + 7))
        def _():
            pl.semaphore_signal(barrier, inc=1, device_id=(end, slab), device_id_type=MESH)
    load = pltpu.make_async_copy(sig, block, load_sem)
    load.start()
    ends = jnp.where(jnp.logical_or(is_a, is_b), 7, 1)
    pl.semaphore_wait(barrier, sum(there.astype(jnp.int32) for there in has) + 1 + ends)

    def leg(src, dst, send, recv, peer):
        return pltpu.make_async_remote_copy(
            src_ref=src, dst_ref=dst, send_sem=send, recv_sem=recv, device_id=(peer, slab), device_id_type=MESH
        )

    def first_legs():
        return (
            [leg(sig.at[j, CY - 1], hop, first_sem.at[j], hop_sem, 2 * j + 1 if j < 3 else 15) for j in range(4)],
            [leg(sig.at[j, 0], hop, first_sem.at[j], hop_sem, 8 + 2 * j if j > 0 else 0) for j in range(4)],
        )

    for at_end, legs in zip((is_a, is_b), first_legs()):
        @pl.when(at_end)
        def _():
            for one in legs:
                one.start()

    early_relay = jnp.logical_and(x + c == 1, jnp.logical_not(jnp.logical_or(is_a, is_b)))
    to_a = jnp.logical_and(x == 0, c == 0)
    to_b = jnp.logical_and(x == 1, c == 1)

    def hop_across():
        return leg(hop, hop, pass_sem, hop_sem, across[0])

    def hop_b():
        return leg(hop, halo.at[2, z], pass_sem, last_sem.at[z], 8)

    def hop_a():
        return leg(hop, halo.at[3, z], pass_sem, last_sem.at[z], 7)

    def halo_copy(d, k):
        lanes = pl.ds(EDGES[k], EDGES[k + 1] - EDGES[k])
        return pltpu.make_async_remote_copy(
            src_ref=planes[d].at[:, :, lanes],
            dst_ref=halo.at[lands[d], :, :, lanes],
            send_sem=send_sem.at[d, k],
            recv_sem=recv_sem.at[lands[d], k],
            device_id=peers[d],
            device_id_type=MESH,
        )

    def halo_wait(d, k):
        lanes = pl.ds(EDGES[k], EDGES[k + 1] - EDGES[k])
        pltpu.make_async_remote_copy(
            src_ref=halo.at[d, :, :, lanes],
            dst_ref=halo.at[d, :, :, lanes],
            send_sem=send_sem.at[d, k],
            recv_sem=recv_sem.at[d, k],
            device_id=peers[d],
            device_id_type=MESH,
        ).wait_recv()

    def send_chunks(chunks):
        for k in chunks:
            for d in range(4):
                @pl.when(has[d])
                def _():
                    halo_copy(d, k).start()

    send_chunks(range(2))

    for d in range(4):
        @pl.when(edge[d])
        def _():
            halo[d] = jnp.zeros_like(halo[d])
    for part in (s_hi, s_lo):
        part[:, 0:REACH] = jnp.zeros((PANEL, REACH), jnp.bfloat16)
        part[:, REACH + FRAMES :] = jnp.zeros((PANEL, REACH), jnp.bfloat16)

    def split(value):
        hi = value.astype(jnp.bfloat16)
        return hi, (value - hi.astype(jnp.float32)).astype(jnp.bfloat16)

    wide = FILTER + 2 * REACH
    lag = lax.broadcasted_iota(jnp.int32, (wide, FILTER), 0) - lax.broadcasted_iota(jnp.int32, (wide, FILTER), 1) - REACH + 4
    band = jnp.zeros((wide, FILTER), jnp.float32)
    for tap in range(9):
        band = jnp.where(lag == tap, taps[tap], band)
    t_hi[...], t_lo[...] = split(band)

    index = jnp.broadcast_to(chosen[...].astype(jnp.float32), (128, PANEL))
    vox[...] = jnp.transpose(index).astype(jnp.int32)
    tall = 64

    def build(t, _):
        at = pl.ds(pl.multiple_of(t * tall, tall), tall)
        v = vox[at, :]
        iota = lax.broadcasted_iota(jnp.int32, (tall, 128), 1)
        iota_z = lax.broadcasted_iota(jnp.int32, (tall, CZ), 1)
        hits = jnp.zeros((tall, CZ), jnp.int32)
        for run in range(CX * CY):
            hits = hits + jnp.where(v[:, :CZ] == iota_z + run * CZ, wclass[run : run + 1, :], 0)
        klass = jnp.sum(hits.astype(jnp.float32), axis=1, keepdims=True)
        weight = []
        for d in range(3):
            w = jnp.zeros_like(klass)
            for c in range(4):
                w = w + jnp.where(klass == float(c), kernel[d, c], 0.0)
            weight.append(jnp.broadcast_to(w, (tall, 128)))
        wx, wy, wz = weight
        centre = 1.0 - 2.0 * (wx + wy + wz)
        x, y, z = v >> 8, (v >> 6) & 3, v & 63
        none = jnp.full_like(v, -1)
        y_lo, y_hi = jnp.where(y > 0, v - CZ, none), jnp.where(y < CY - 1, v + CZ, none)
        z_lo, z_hi = jnp.where(z > 0, v - 1, none), jnp.where(z < CZ - 1, v + 1, none)
        plane = x * CZ + z

        def put(column, w):
            w_hi[at, column : column + 128], w_lo[at, column : column + 128] = split(w)

        zero = jnp.zeros((tall, 128), jnp.float32)
        for b in range(VOXELS // 128):
            col = iota + b * 128
            w = jnp.where(col == v, centre, zero)
            w = jnp.where((col == v - 256) | (col == v + 256), wx, w)
            w = jnp.where((col == y_lo) | (col == y_hi), wy, w)
            put(b * 128, jnp.where((col == z_lo) | (col == z_hi), wz, w))
        picks = (
            (v, wx),
            (v - 768, wx),
            (jnp.where(y == 0, plane, none), wy),
            (jnp.where(y == CY - 1, plane, none), wy),
        )
        for d, (pick, w) in enumerate(picks):
            for b in range(2):
                put(VOXELS + d * 256 + b * 128, jnp.where(iota + b * 128 == pick, w, zero))
        return 0

    lax.fori_loop(0, PANEL // tall, build, 0)

    @pl.when(early_relay)
    def _():
        hop_across().wait_recv()
        hop_across().start()

    send_chunks(range(2, CHUNKS))

    half = 256

    def product(ref, first, lanes, h):
        at = pl.ds(pl.multiple_of(h * half, half), half)
        right = ref[:, :, :, lanes].reshape(VOXELS, -1)
        cols = pl.ds(first, VOXELS)
        return jnp.dot(w_hi[at, cols], right, preferred_element_type=jnp.float32) + jnp.dot(
            w_lo[at, cols], right, preferred_element_type=jnp.float32
        )

    load.wait()

    def inner(i, _):
        k, h = i // 2, i % 2
        at = pl.ds(pl.multiple_of(h * half, half), half)
        lanes = pl.ds(pl.multiple_of(k * WIDE, 128), WIDE)
        filt[at, lanes] = product(block, 0, lanes, h)
        return 0

    lax.fori_loop(0, FRAMES // WIDE * 2, inner, 0)
    sums[...] = jnp.zeros_like(sums)

    for relay, onward in ((to_a, hop_a), (to_b, hop_b)):
        @pl.when(relay)
        def _():
            hop_across().wait_recv()
            onward().start()

    for at_end, onward in ((is_a, 3), (is_b, 2)):
        @pl.when(at_end)
        def _():
            for j in range(4):
                leg(hop, halo.at[onward, j], pass_sem, last_sem.at[j], 7).wait_recv()

    def filter_part(at, first, width):
        window = pl.ds(first, width + 2 * REACH)
        hi, lo = s_hi[at, window], s_lo[at, window]
        rows_of = pl.ds(0, width + 2 * REACH)
        cols = pl.ds(0, width)
        a, b = t_hi[rows_of, cols], t_lo[rows_of, cols]
        total = jnp.dot(hi, a, preferred_element_type=jnp.float32)
        total = total + jnp.dot(hi, b, preferred_element_type=jnp.float32)
        total = total + jnp.dot(lo, a, preferred_element_type=jnp.float32)
        filt[at, pl.ds(first, width)] = total
        for i in range(width // 128):
            sums[at, :] += total[:, i * 128 : (i + 1) * 128]

    for k in range(CHUNKS):
        for d in range(4):
            @pl.when(has[d])
            def _():
                halo_wait(d, k)

        lanes = pl.ds(EDGES[k], EDGES[k + 1] - EDGES[k])
        shifted = pl.ds(EDGES[k] + REACH, EDGES[k + 1] - EDGES[k])
        first = max(0, EDGES[k] - REACH)
        last = FRAMES if k == CHUNKS - 1 else EDGES[k + 1] - REACH

        def outer(h, _):
            at = pl.ds(pl.multiple_of(h * half, half), half)
            s_hi[at, shifted], s_lo[at, shifted] = split(filt[at, lanes] + product(halo, VOXELS, lanes, h))
            for start in range(first, last, FILTER):
                filter_part(at, start, min(FILTER, last - start))
            return 0

        lax.fori_loop(0, 2, outer, 0)

    deep = 64

    def norm(t, _):
        at = pl.ds(pl.multiple_of(t * deep, deep), deep)
        mean = jnp.sum(sums[at, :], axis=1, keepdims=True) * (1.0 / FRAMES)
        wide_mean = jnp.broadcast_to(mean, (deep, 128))
        square = jnp.zeros((deep, 128), jnp.float32)
        for i in range(FRAMES // 128):
            centred = filt[at, i * 128 : (i + 1) * 128] - wide_mean
            square = square + centred * centred
        scale = lax.rsqrt(jnp.sum(square, axis=1, keepdims=True) * (1.0 / FRAMES) + 1e-05)
        wide_scale = jnp.broadcast_to(scale, (deep, 128))
        for i in range(FRAMES // 128):
            lanes = slice(i * 128, (i + 1) * 128)
            rows[at, lanes] = ((filt[at, lanes] - wide_mean) * wide_scale).astype(jnp.bfloat16)
        return 0

    lax.fori_loop(0, PANEL // deep, norm, 0)

    for at_end, legs in zip((is_a, is_b), first_legs()):
        @pl.when(at_end)
        def _():
            for one in legs:
                one.wait_send()

    @pl.when(jnp.logical_not(jnp.logical_or(is_a, is_b)))
    def _():
        hop_across().wait_send()

    for k in range(CHUNKS):
        for d in range(4):
            @pl.when(has[d])
            def _():
                halo_copy(d, k).wait_send()


def front(signal, chosen, wclass, kernel, taps):
    vmem = pl.BlockSpec(memory_space=pltpu.VMEM)
    smem = pl.BlockSpec(memory_space=pltpu.SMEM)
    return pl.pallas_call(
        front_kernel,
        out_shape=pltpu.VMEM((PANEL, FRAMES), jnp.bfloat16),
        in_specs=[pl.BlockSpec(memory_space=pl.ANY), vmem, vmem, smem, smem],
        out_specs=vmem,
        scratch_shapes=[
            pltpu.VMEM((CX, CY, CZ, FRAMES), jnp.bfloat16),
            pltpu.VMEM((4, 4, CZ, FRAMES), jnp.bfloat16),
            pltpu.VMEM((PANEL, 128), jnp.int32),
            pltpu.VMEM((PANEL, 2 * VOXELS), jnp.bfloat16),
            pltpu.VMEM((PANEL, 2 * VOXELS), jnp.bfloat16),
            pltpu.VMEM((PANEL, FRAMES + 2 * REACH), jnp.bfloat16),
            pltpu.VMEM((PANEL, FRAMES + 2 * REACH), jnp.bfloat16),
            pltpu.VMEM((FILTER + 2 * REACH, FILTER), jnp.bfloat16),
            pltpu.VMEM((FILTER + 2 * REACH, FILTER), jnp.bfloat16),
            pltpu.VMEM((PANEL, FRAMES), jnp.float32),
            pltpu.VMEM((PANEL, 128), jnp.float32),
            pltpu.VMEM((CZ, FRAMES), jnp.bfloat16),
            pltpu.SemaphoreType.DMA,
            pltpu.SemaphoreType.DMA((4, CHUNKS)),
            pltpu.SemaphoreType.DMA((4, CHUNKS)),
            pltpu.SemaphoreType.DMA((4,)),
            pltpu.SemaphoreType.DMA,
            pltpu.SemaphoreType.DMA,
            pltpu.SemaphoreType.DMA((4,)),
        ],
        compiler_params=pltpu.CompilerParams(
            collective_id=0, has_side_effects=True, vmem_limit_bytes=56 * 2**20
        ),
        name="front",
    )(signal, chosen, wclass, kernel, taps)


def correlate(left, right):
    product = lax.dot_general(
        left.reshape(PANEL, FRAMES), right, (((1,), (1,)), ((), ())), preferred_element_type=jnp.float32
    )
    return product * (1.0 / FRAMES**0.5)


def interleave(h, same, opposite):
    low, high = jnp.where(h == 0, same, opposite), jnp.where(h == 0, opposite, same)
    lane = lax.broadcasted_iota(jnp.int32, (PANEL, 128), 1)
    parts = []
    for i in range(2):
        a, b = low[:, i * 128 : (i + 1) * 128], high[:, i * 128 : (i + 1) * 128]
        parts.append(jnp.where(lane < 64, a, pltpu.roll(b, 64, axis=1)).astype(jnp.bfloat16))
        parts.append(jnp.where(lane < 64, pltpu.roll(a, 64, axis=1), b).astype(jnp.bfloat16))
    return parts


def group_kernel(rows, tiles, own, far_rest, far_part, held, x_out, x_in, z_out, z_in, swap_sem, x_sem, mate_sem, mirror_sem, core_sem, recv_sem, lend_sem, borrow_sem, own_sem):
    loop, slab = lax.axis_index("loop"), lax.axis_index("slab")
    x, z, c = loop // 8, (loop // 2) % 4, loop % 2
    y, h = slab // 2, slab % 2
    z_mate, z_mirror, z_far = z + 1 - 2 * (z % 2), 3 - z, (z + 2) % 4

    def panel(px, pz, pc=None):
        return px * 8 + pz * 2 + (c if pc is None else pc)

    mate, mirror = (panel(x, z_mate), slab), (panel(x, z_mirror), slab)
    across, sibling = (panel(1 - x, z), slab), (panel(x, z, 1 - c), slab)
    inside = [(loop, ((y + dy) % 4) * 2 + h) for dy in (1, 3, 2)]
    outside = [(panel(1 - x, z), ((y + dy) % 4) * 2 + 1 - h) for dy in ORDER]

    barrier = pltpu.get_barrier_semaphore()
    peers = [mate, mirror, across, sibling] + inside + outside
    for peer in peers:
        pl.semaphore_signal(barrier, inc=1, device_id=peer, device_id_type=MESH)
    pl.semaphore_wait(barrier, len(peers))

    def at(p):
        dy = jnp.where(p == 2, 3, jnp.where(p == 3, 2, p))
        return (y + dy) % 4

    def copy(q, py, ph, sem, peer):
        return pltpu.make_async_remote_copy(
            src_ref=held.at[q, py, ph],
            dst_ref=held.at[q, py, ph],
            send_sem=sem.at[q, py, ph],
            recv_sem=recv_sem.at[q, py, ph],
            device_id=peer,
            device_id_type=MESH,
        )

    def copy_far(q, py, sem, peer, src):
        return pltpu.make_async_remote_copy(
            src_ref=src,
            dst_ref=far_rest.at[c, py],
            send_sem=sem.at[q, py, 1 - h],
            recv_sem=recv_sem.at[q, py, 1 - h],
            device_id=peer,
            device_id_type=MESH,
        )

    def arrived(q, py, ph):
        copy(q, py, ph, core_sem, sibling).wait_recv()

    swaps = []
    for i, peer in enumerate(outside + inside):
        to_y, to_h = peer[1] // 2, peer[1] % 2
        swaps.append(pltpu.make_async_remote_copy(
            src_ref=rows.at[to_y, to_h],
            dst_ref=held.at[loop, y, h],
            send_sem=swap_sem.at[i],
            recv_sem=recv_sem.at[loop, y, h],
            device_id=peer,
            device_id_type=MESH,
        ))
    pltpu.make_async_copy(rows.at[y, h], held.at[loop, y, h], recv_sem.at[loop, y, h]).start()
    for i in (0, 4, 1, 5, 2, 6, 3):
        swaps[i].start()

    mine, other = panel(x, z), panel(1 - x, z)

    def own_rest(p):
        py = at(p)
        arrived(mine, py, 1 - h)
        copy(mine, py, 1 - h, mirror_sem, mirror).start()
        copy(mine, py, 1 - h, core_sem, sibling).start()

    def own_first(p):
        py = at(p)
        copy(mine, py, h, mirror_sem, mirror).start()
        copy(mine, py, h, mate_sem, mate).start()
        copy(mine, py, h, core_sem, sibling).start()

    pltpu.make_async_copy(rows.at[y, h], held.at[loop, y, h], recv_sem.at[loop, y, h]).wait()
    copy(mine, y, h, x_sem, across).start()
    own_first(0)

    def straight(p, _):
        arrived(mine, at(p), h)
        own_first(p)
        return 0

    lax.fori_loop(1, 3, straight, 0)

    def begin(p, _):
        py = at(p)

        @pl.when(p >= 2)
        def _():
            own_rest(p - 2)
        arrived(other, py, 1 - h)
        copy(other, py, 1 - h, x_sem, across).start()
        copy(other, py, 1 - h, mate_sem, mate).start()
        copy(other, py, 1 - h, core_sem, sibling).start()

        @pl.when(p == 2)
        def _():
            copy(mine, at(1), h, x_sem, across).start()
            straight(3, 0)
        return 0

    lax.fori_loop(0, 4, begin, 0)
    copy(mine, at(2), h, x_sem, across).start()
    copy(mine, at(3), h, x_sem, across).start()

    def onward(p, q, odd, rest):
        sem, peer = (mate_sem, mate) if odd else (mirror_sem, mirror)

        @pl.when(p % 2 == odd)
        def _():
            if rest:
                copy_far(q, at(p), sem, peer, held.at[q, at(p), 1 - h]).start()
            else:
                copy(q, at(p), h, sem, peer).start()

    def second(p, _):
        py = at(p)
        for pz, odd in ((z_mirror, 1), (z_mate, 0)):
            q = panel(x, pz)
            arrived(q, py, h)
            onward(p, q, odd, False)
            copy(q, py, h, core_sem, sibling).start()
        q = panel(1 - x, z_mate)
        arrived(q, py, 1 - h)
        copy(q, py, 1 - h, core_sem, sibling).start()
        return 0

    own_rest(2)
    lax.fori_loop(0, 4, second, 0)
    own_rest(3)

    def rest_to_mate(p, _):
        copy(mine, at(p), 1 - h, mate_sem, mate).start()
        return 0

    lax.fori_loop(0, 4, rest_to_mate, 0)

    def came_across(p, _):
        arrived(other, at(p), h)
        copy(other, at(p), h, core_sem, sibling).start()
        return 0

    lax.fori_loop(0, 4, came_across, 0)

    def from_sibling(px, pz, ph):
        def body(p, _):
            arrived(panel(px, pz, 1 - c), at(p), ph)
            return 0

        lax.fori_loop(0, 4, body, 0)

    def times(q, right):
        return correlate(held[q], right)

    def half(q, ph):
        return held[q, :, ph].reshape(PANEL // 2, FRAMES)

    def lend(axis, j, pc):
        out, into, peer = ((x_out, x_in, across), (z_out, z_in, mirror))[axis]
        return pltpu.make_async_remote_copy(
            src_ref=out.at[j, pc],
            dst_ref=into.at[j, pc],
            send_sem=lend_sem.at[axis, j, pc],
            recv_sem=borrow_sem.at[axis, j, pc],
            device_id=peer,
            device_id_type=MESH,
        )

    def lend_across(j, pz):
        from_sibling(x, pz, h)

        def body(pc, _):
            x_out[j, pc] = times(other, half(panel(x, pz, pc), h)).astype(jnp.bfloat16)
            lend(0, j, pc).start()
            return 0

        lax.fori_loop(0, 2, body, 0)

    def lend_mirror(j, pz):
        from_sibling(1 - x, pz, 1 - h)

        def body(pc, _):
            z_out[j, pc] = times(panel(x, z_mirror), half(panel(1 - x, pz, pc), 1 - h)).astype(jnp.bfloat16)
            lend(1, j, pc).start()
            return 0

        lax.fori_loop(0, 2, body, 0)

    def columns(q, first, width):
        return pl.ds(pl.multiple_of(q * PANEL + first, 128), width)

    def full(px, pz):
        def body(i, _):
            q, j = panel(px, pz, i // 2), i % 2
            right = held[q, pl.ds(2 * j, 2)].reshape(PANEL // 2, FRAMES)
            tiles[:, columns(q, j * 256, 256)] = times(loop, right).astype(jnp.bfloat16)
            return 0

        lax.fori_loop(0, 4, body, 0)

    def place(q, same, opposite):
        for i, part in enumerate(interleave(h, same, opposite)):
            tiles[:, columns(q, i * 128, 128)] = part

    def borrowed(axis, j, pc):
        lend(axis, j, pc).wait_recv()
        return (x_in, z_in)[axis][j, pc].astype(jnp.float32)

    def each_core(body):
        def step(pc, _):
            body(pc)
            return 0

        lax.fori_loop(0, 2, step, 0)

    def early_across(j, _):
        lend_across(j, jnp.where(j == 0, z_mirror, z_mate))
        return 0

    lax.fori_loop(0, 2, early_across, 0)

    def third(p, _):
        q = panel(x, z_mirror)
        arrived(q, at(p), 1 - h)
        onward(p, q, 1, True)
        copy(q, at(p), 1 - h, core_sem, sibling).start()
        return 0

    lax.fori_loop(0, 4, third, 0)

    def to_mirror(j, _):
        lend_mirror(j, jnp.where(j == 0, z, z_mate))
        return 0

    lax.fori_loop(0, 2, to_mirror, 0)

    keep = pltpu.make_async_copy(held.at[loop], own, own_sem)
    keep.start()
    from_sibling(x, z, 0)
    from_sibling(x, z, 1)
    full(x, z)

    def from_far(p, _):
        q = panel(x, z_far)
        arrived(q, at(p), h)
        copy(q, at(p), h, core_sem, sibling).start()
        return 0

    lax.fori_loop(0, 4, from_far, 0)
    lend_across(2, z_far)
    from_sibling(1 - x, z, h)
    full(1 - x, z)

    def fourth(p, _):
        q = panel(x, z_mate)
        arrived(q, at(p), 1 - h)
        onward(p, q, 0, True)
        copy(q, at(p), 1 - h, core_sem, sibling).start()
        return 0

    lax.fori_loop(0, 4, fourth, 0)

    from_sibling(x, z_mirror, 1 - h)
    from_sibling(x, z_mate, 1 - h)

    def whole(i, _):
        full(x, jnp.where(i == 0, z_mirror, z_mate))
        return 0

    lax.fori_loop(0, 2, whole, 0)

    def part_mate(pc):
        q = panel(1 - x, z_mate, pc)
        place(q, borrowed(0, 1, pc), times(loop, half(q, 1 - h)))

    def none_mirror(pc):
        place(panel(1 - x, z_mirror, pc), borrowed(0, 0, pc), borrowed(1, 0, pc))

    def none_far(pc):
        place(panel(1 - x, z_far, pc), borrowed(0, 2, pc), borrowed(1, 1, pc))

    def first_far(pc):
        far_part[pc] = times(loop, half(panel(x, z_far, pc), h)).astype(jnp.bfloat16)

    each_core(part_mate)
    each_core(first_far)
    each_core(none_mirror)

    def fifth(p, _):
        q = panel(x, z_far)
        arrived(q, at(p), 1 - h)
        copy_far(q, at(p), core_sem, sibling, far_rest.at[c, at(p)]).start()
        return 0

    lax.fori_loop(0, 4, fifth, 0)
    each_core(none_far)

    from_sibling(x, z_far, 1 - h)

    keep.wait()
    for swap in swaps:
        swap.wait_send()
    for axis, count in ((0, 3), (1, 2)):
        for j in range(count):
            for pc in range(2):
                lend(axis, j, pc).wait_send()

    def left(p, _):
        py = at(p)
        for q, ph in ((mine, h), (mine, 1 - h), (other, 1 - h)):
            copy(q, py, ph, mate_sem, mate).wait_send()
        for q, ph in ((mine, h), (mine, 1 - h)):
            copy(q, py, ph, mirror_sem, mirror).wait_send()
        for q, ph in ((mine, h), (other, 1 - h)):
            copy(q, py, ph, x_sem, across).wait_send()

        for ph in range(2):
            @pl.when(p % 2 == 1)
            def _():
                copy(panel(x, z_mirror), py, ph, mate_sem, mate).wait_send()

            @pl.when(p % 2 == 0)
            def _():
                copy(panel(x, z_mate), py, ph, mirror_sem, mirror).wait_send()
            for q in (mine, other, panel(x, z_mate), panel(x, z_mirror)):
                copy(q, py, ph, core_sem, sibling).wait_send()
        copy(panel(x, z_far), py, h, core_sem, sibling).wait_send()
        copy_far(panel(x, z_far), py, core_sem, sibling, far_rest.at[c, py]).wait_send()
        copy(panel(1 - x, z_mate), py, 1 - h, core_sem, sibling).wait_send()
        return 0

    lax.fori_loop(0, 4, left, 0)


def group(rows):
    block = (N_LOOP, 4, 2)
    part = (2, PANEL, PANEL // 2)
    return pl.pallas_call(
        group_kernel,
        out_shape=(
            pltpu.VMEM((PANEL, N_LOOP * PANEL), jnp.bfloat16),
            pltpu.VMEM((4, 2, SHARE, FRAMES), jnp.bfloat16),
            pltpu.VMEM((2, 4, SHARE, FRAMES), jnp.bfloat16),
            pltpu.VMEM(part, jnp.bfloat16),
        ),
        in_specs=[pl.BlockSpec(memory_space=pl.ANY)],
        out_specs=(pl.BlockSpec(memory_space=pltpu.VMEM),) * 4,
        scratch_shapes=[pltpu.VMEM(block + (SHARE, FRAMES), jnp.bfloat16)]
        + [pltpu.VMEM((count,) + part, jnp.bfloat16) for count in (3, 3, 2, 2)]
        + [pltpu.SemaphoreType.DMA((7,))]
        + [pltpu.SemaphoreType.DMA(block)] * 5
        + [pltpu.SemaphoreType.DMA((2, 3, 2))] * 2
        + [pltpu.SemaphoreType.DMA],
        compiler_params=pltpu.CompilerParams(
            collective_id=1, has_side_effects=True, vmem_limit_bytes=40 * 2**20
        ),
        name="group",
    )(pltpu.with_memory_space_constraint(rows, pltpu.VMEM))


def finish_kernel(tiles, own, far_rest, far_part, out, stage, sems):
    loop, h = lax.axis_index("loop"), lax.axis_index("slab") % 2
    far = loop // 8 * 4 + (loop // 2 + 2) % 4
    wide = 2 * PANEL

    def columns(pair):
        return pl.ds(pl.multiple_of(pair * wide, wide), wide)

    def ready(i):
        pair = (far + 1 + i) % 8
        return pltpu.make_async_copy(tiles.at[:, columns(pair)], out.at[:, columns(pair)], sems.at[i])

    for i in range(7):
        ready(i).start()

    def body(pc, _):
        right = far_rest[pc].reshape(PANEL // 2, FRAMES)
        parts = interleave(h, far_part[pc].astype(jnp.float32), correlate(own[...], right))
        for i, part in enumerate(parts):
            stage[:, pl.ds(pl.multiple_of(pc * PANEL + i * 128, 128), 128)] = part
        return 0

    lax.fori_loop(0, 2, body, 0)
    last = pltpu.make_async_copy(stage, out.at[:, columns(far)], sems.at[7])
    last.start()
    for i in range(7):
        ready(i).wait()
    last.wait()


def finish(tiles, own, far_rest, far_part):
    return pl.pallas_call(
        finish_kernel,
        out_shape=jax.ShapeDtypeStruct((PANEL, N_LOOP * PANEL), jnp.bfloat16),
        in_specs=[pl.BlockSpec(memory_space=pl.ANY)] + [pl.BlockSpec(memory_space=pltpu.VMEM)] * 3,
        out_specs=pl.BlockSpec(memory_space=pl.ANY),
        scratch_shapes=[pltpu.VMEM((PANEL, 2 * PANEL), jnp.bfloat16), pltpu.SemaphoreType.DMA((8,))],
        compiler_params=pltpu.CompilerParams(vmem_limit_bytes=12 * 2**20),
        name="finish",
    )(*(pltpu.with_memory_space_constraint(array, pltpu.VMEM) for array in (tiles, own, far_rest, far_part)))


def local(signal, width_class, kernel, taps, chosen):
    rows = front(signal, chosen.reshape(1, PANEL), width_class.reshape(CX * CY, CZ), kernel, taps)
    wide = finish(*group(rows.reshape(4, 2, SHARE, FRAMES)))
    return wide.reshape(PANEL, 1, N_LOOP * PANEL)


def solution(mesh):
    in_specs = (
        P("slab", "loop", None, None),
        P("slab", "loop", None),
        P(),
        P(),
        P("loop", "slab", None),
    )
    return jax.shard_map(local, mesh=mesh, in_specs=in_specs, out_specs=P("loop", "slab", None), check_vma=False)
```

```python
import functools

import jax
import jax.numpy as jnp
from jax import lax
from jax.experimental import pallas as pl
from jax.experimental.pallas import tpu as pltpu
from jax.sharding import PartitionSpec as P

MESH = pl.DeviceIdType.MESH
CX, CY, CZ, FRAMES = 4, 4, 64, 1920
VOXELS = CX * CY * CZ
PANEL = 512
SHARE = 64
N_LOOP, N_SLAB = 16, 8
EDGES = (0, 384, 896, 1408, 1664, 1920)
CHUNKS = len(EDGES) - 1
WIDE = 384
REACH = 128
FILTER = 256
ORDER = (0, 1, 3, 2)


def front_kernel(sig, chosen, wclass, kernel, taps, rows, block, halo, vox, w_hi, w_lo, s_hi, s_lo, t_hi, t_lo, filt, sums, hop, load_sem, send_sem, recv_sem, first_sem, pass_sem, hop_sem, last_sem):
    loop, slab = lax.axis_index("loop"), lax.axis_index("slab")
    x, z, c = loop // 8, (loop // 2) % 4, loop % 2
    is_a, is_b = loop == 7, loop == 8
    has = (slab > 0, slab < N_SLAB - 1, jnp.logical_and(loop > 0, loop != 8), jnp.logical_and(loop < N_LOOP - 1, loop != 7))
    edge = (slab == 0, slab == N_SLAB - 1, loop == 0, loop == N_LOOP - 1)
    peers = ((loop, slab - 1), (loop, slab + 1), (loop - 1, slab), (loop + 1, slab))
    planes = (sig.at[0], sig.at[CX - 1], sig.at[:, 0], sig.at[:, CY - 1])
    lands = (1, 0, 3, 2)

    barrier = pltpu.get_barrier_semaphore()
    for there, peer in zip(has, peers):
        @pl.when(there)
        def _():
            pl.semaphore_signal(barrier, inc=1, device_id=peer, device_id_type=MESH)
    across = ((loop + 8) % N_LOOP, slab)
    pl.semaphore_signal(barrier, inc=1, device_id=across, device_id_type=MESH)
    for at_end, end in ((is_a, 7), (is_b, 8)):
        low = 0 if end == 7 else 9

        @pl.when(at_end)
        def _():
            for there in range(low, low + 7):
                pl.semaphore_signal(barrier, inc=1, device_id=(there, slab), device_id_type=MESH)

        @pl.when(jnp.logical_and(loop >= low, loop < low + 7))
        def _():
            pl.semaphore_signal(barrier, inc=1, device_id=(end, slab), device_id_type=MESH)
    load = pltpu.make_async_copy(sig, block, load_sem)
    load.start()
    ends = jnp.where(jnp.logical_or(is_a, is_b), 7, 1)
    pl.semaphore_wait(barrier, sum(there.astype(jnp.int32) for there in has) + 1 + ends)

    def leg(src, dst, send, recv, peer):
        return pltpu.make_async_remote_copy(
            src_ref=src, dst_ref=dst, send_sem=send, recv_sem=recv, device_id=(peer, slab), device_id_type=MESH
        )

    def first_legs():
        return (
            [leg(sig.at[j, CY - 1], hop, first_sem.at[j], hop_sem, 2 * j + 1 if j < 3 else 15) for j in range(4)],
            [leg(sig.at[j, 0], hop, first_sem.at[j], hop_sem, 8 + 2 * j if j > 0 else 0) for j in range(4)],
        )

    for at_end, legs in zip((is_a, is_b), first_legs()):
        @pl.when(at_end)
        def _():
            for one in legs:
                one.start()

    early_relay = jnp.logical_and(x + c == 1, jnp.logical_not(jnp.logical_or(is_a, is_b)))
    to_a = jnp.logical_and(x == 0, c == 0)
    to_b = jnp.logical_and(x == 1, c == 1)

    def hop_across():
        return leg(hop, hop, pass_sem, hop_sem, across[0])

    def hop_b():
        return leg(hop, halo.at[2, z], pass_sem, last_sem.at[z], 8)

    def hop_a():
        return leg(hop, halo.at[3, z], pass_sem, last_sem.at[z], 7)

    def halo_copy(d, k):
        lanes = pl.ds(EDGES[k], EDGES[k + 1] - EDGES[k])
        return pltpu.make_async_remote_copy(
            src_ref=planes[d].at[:, :, lanes],
            dst_ref=halo.at[lands[d], :, :, lanes],
            send_sem=send_sem.at[d, k],
            recv_sem=recv_sem.at[lands[d], k],
            device_id=peers[d],
            device_id_type=MESH,
        )

    def halo_wait(d, k):
        lanes = pl.ds(EDGES[k], EDGES[k + 1] - EDGES[k])
        pltpu.make_async_remote_copy(
            src_ref=halo.at[d, :, :, lanes],
            dst_ref=halo.at[d, :, :, lanes],
            send_sem=send_sem.at[d, k],
            recv_sem=recv_sem.at[d, k],
            device_id=peers[d],
            device_id_type=MESH,
        ).wait_recv()

    def send_chunks(chunks):
        for k in chunks:
            for d in range(4):
                @pl.when(has[d])
                def _():
                    halo_copy(d, k).start()

    send_chunks(range(2))

    for d in range(4):
        @pl.when(edge[d])
        def _():
            halo[d] = jnp.zeros_like(halo[d])
    for part in (s_hi, s_lo):
        part[:, 0:REACH] = jnp.zeros((PANEL, REACH), jnp.bfloat16)
        part[:, REACH + FRAMES :] = jnp.zeros((PANEL, REACH), jnp.bfloat16)

    def split(value):
        hi = value.astype(jnp.bfloat16)
        return hi, (value - hi.astype(jnp.float32)).astype(jnp.bfloat16)

    wide = FILTER + 2 * REACH
    lag = lax.broadcasted_iota(jnp.int32, (wide, FILTER), 0) - lax.broadcasted_iota(jnp.int32, (wide, FILTER), 1) - REACH + 4
    band = jnp.zeros((wide, FILTER), jnp.float32)
    for tap in range(9):
        band = jnp.where(lag == tap, taps[tap], band)
    t_hi[...], t_lo[...] = split(band)

    index = jnp.broadcast_to(chosen[...].astype(jnp.float32), (128, PANEL))
    vox[...] = jnp.transpose(index).astype(jnp.int32)
    tall = 64

    def build(t, _):
        at = pl.ds(pl.multiple_of(t * tall, tall), tall)
        v = vox[at, :]
        iota = lax.broadcasted_iota(jnp.int32, (tall, 128), 1)
        iota_z = lax.broadcasted_iota(jnp.int32, (tall, CZ), 1)
        hits = jnp.zeros((tall, CZ), jnp.int32)
        for run in range(CX * CY):
            hits = hits + jnp.where(v[:, :CZ] == iota_z + run * CZ, wclass[run : run + 1, :], 0)
        klass = jnp.sum(hits.astype(jnp.float32), axis=1, keepdims=True)
        weight = []
        for d in range(3):
            w = jnp.zeros_like(klass)
            for c in range(4):
                w = w + jnp.where(klass == float(c), kernel[d, c], 0.0)
            weight.append(jnp.broadcast_to(w, (tall, 128)))
        wx, wy, wz = weight
        centre = 1.0 - 2.0 * (wx + wy + wz)
        x, y, z = v >> 8, (v >> 6) & 3, v & 63
        none = jnp.full_like(v, -1)
        y_lo, y_hi = jnp.where(y > 0, v - CZ, none), jnp.where(y < CY - 1, v + CZ, none)
        z_lo, z_hi = jnp.where(z > 0, v - 1, none), jnp.where(z < CZ - 1, v + 1, none)
        plane = x * CZ + z

        def put(column, w):
            w_hi[at, column : column + 128], w_lo[at, column : column + 128] = split(w)

        zero = jnp.zeros((tall, 128), jnp.float32)
        for b in range(VOXELS // 128):
            col = iota + b * 128
            w = jnp.where(col == v, centre, zero)
            w = jnp.where((col == v - 256) | (col == v + 256), wx, w)
            w = jnp.where((col == y_lo) | (col == y_hi), wy, w)
            put(b * 128, jnp.where((col == z_lo) | (col == z_hi), wz, w))
        picks = (
            (v, wx),
            (v - 768, wx),
            (jnp.where(y == 0, plane, none), wy),
            (jnp.where(y == CY - 1, plane, none), wy),
        )
        for d, (pick, w) in enumerate(picks):
            for b in range(2):
                put(VOXELS + d * 256 + b * 128, jnp.where(iota + b * 128 == pick, w, zero))
        return 0

    lax.fori_loop(0, PANEL // tall, build, 0)

    @pl.when(early_relay)
    def _():
        hop_across().wait_recv()
        hop_across().start()

    send_chunks(range(2, CHUNKS))

    half = 256

    def product(ref, first, lanes, h):
        at = pl.ds(pl.multiple_of(h * half, half), half)
        right = ref[:, :, :, lanes].reshape(VOXELS, -1)
        cols = pl.ds(first, VOXELS)
        return jnp.dot(w_hi[at, cols], right, preferred_element_type=jnp.float32) + jnp.dot(
            w_lo[at, cols], right, preferred_element_type=jnp.float32
        )

    load.wait()

    def inner(i, _):
        k, h = i // 2, i % 2
        at = pl.ds(pl.multiple_of(h * half, half), half)
        lanes = pl.ds(pl.multiple_of(k * WIDE, 128), WIDE)
        filt[at, lanes] = product(block, 0, lanes, h)
        return 0

    lax.fori_loop(0, FRAMES // WIDE * 2, inner, 0)
    sums[...] = jnp.zeros_like(sums)

    for relay, onward in ((to_a, hop_a), (to_b, hop_b)):
        @pl.when(relay)
        def _():
            hop_across().wait_recv()
            onward().start()

    for at_end, onward in ((is_a, 3), (is_b, 2)):
        @pl.when(at_end)
        def _():
            for j in range(4):
                leg(hop, halo.at[onward, j], pass_sem, last_sem.at[j], 7).wait_recv()

    def filter_part(at, first, width):
        window = pl.ds(first, width + 2 * REACH)
        hi, lo = s_hi[at, window], s_lo[at, window]
        rows_of = pl.ds(0, width + 2 * REACH)
        cols = pl.ds(0, width)
        a, b = t_hi[rows_of, cols], t_lo[rows_of, cols]
        total = jnp.dot(hi, a, preferred_element_type=jnp.float32)
        total = total + jnp.dot(hi, b, preferred_element_type=jnp.float32)
        total = total + jnp.dot(lo, a, preferred_element_type=jnp.float32)
        filt[at, pl.ds(first, width)] = total
        for i in range(width // 128):
            sums[at, :] += total[:, i * 128 : (i + 1) * 128]

    for k in range(CHUNKS):
        for d in range(4):
            @pl.when(has[d])
            def _():
                halo_wait(d, k)

        lanes = pl.ds(EDGES[k], EDGES[k + 1] - EDGES[k])
        shifted = pl.ds(EDGES[k] + REACH, EDGES[k + 1] - EDGES[k])
        first = max(0, EDGES[k] - REACH)
        last = FRAMES if k == CHUNKS - 1 else EDGES[k + 1] - REACH

        def outer(h, _):
            at = pl.ds(pl.multiple_of(h * half, half), half)
            s_hi[at, shifted], s_lo[at, shifted] = split(filt[at, lanes] + product(halo, VOXELS, lanes, h))
            for start in range(first, last, FILTER):
                filter_part(at, start, min(FILTER, last - start))
            return 0

        lax.fori_loop(0, 2, outer, 0)

    deep = 64

    def norm(t, _):
        at = pl.ds(pl.multiple_of(t * deep, deep), deep)
        mean = jnp.sum(sums[at, :], axis=1, keepdims=True) * (1.0 / FRAMES)
        wide_mean = jnp.broadcast_to(mean, (deep, 128))
        square = jnp.zeros((deep, 128), jnp.float32)
        for i in range(FRAMES // 128):
            centred = filt[at, i * 128 : (i + 1) * 128] - wide_mean
            square = square + centred * centred
        scale = lax.rsqrt(jnp.sum(square, axis=1, keepdims=True) * (1.0 / FRAMES) + 1e-05)
        wide_scale = jnp.broadcast_to(scale, (deep, 128))
        for i in range(FRAMES // 128):
            lanes = slice(i * 128, (i + 1) * 128)
            rows[at, lanes] = ((filt[at, lanes] - wide_mean) * wide_scale).astype(jnp.bfloat16)
        return 0

    lax.fori_loop(0, PANEL // deep, norm, 0)

    for at_end, legs in zip((is_a, is_b), first_legs()):
        @pl.when(at_end)
        def _():
            for one in legs:
                one.wait_send()

    @pl.when(jnp.logical_not(jnp.logical_or(is_a, is_b)))
    def _():
        hop_across().wait_send()

    for k in range(CHUNKS):
        for d in range(4):
            @pl.when(has[d])
            def _():
                halo_copy(d, k).wait_send()


def front(signal, chosen, wclass, kernel, taps):
    vmem = pl.BlockSpec(memory_space=pltpu.VMEM)
    smem = pl.BlockSpec(memory_space=pltpu.SMEM)
    return pl.pallas_call(
        front_kernel,
        out_shape=pltpu.VMEM((PANEL, FRAMES), jnp.bfloat16),
        in_specs=[pl.BlockSpec(memory_space=pl.ANY), vmem, vmem, smem, smem],
        out_specs=vmem,
        scratch_shapes=[
            pltpu.VMEM((CX, CY, CZ, FRAMES), jnp.bfloat16),
            pltpu.VMEM((4, 4, CZ, FRAMES), jnp.bfloat16),
            pltpu.VMEM((PANEL, 128), jnp.int32),
            pltpu.VMEM((PANEL, 2 * VOXELS), jnp.bfloat16),
            pltpu.VMEM((PANEL, 2 * VOXELS), jnp.bfloat16),
            pltpu.VMEM((PANEL, FRAMES + 2 * REACH), jnp.bfloat16),
            pltpu.VMEM((PANEL, FRAMES + 2 * REACH), jnp.bfloat16),
            pltpu.VMEM((FILTER + 2 * REACH, FILTER), jnp.bfloat16),
            pltpu.VMEM((FILTER + 2 * REACH, FILTER), jnp.bfloat16),
            pltpu.VMEM((PANEL, FRAMES), jnp.float32),
            pltpu.VMEM((PANEL, 128), jnp.float32),
            pltpu.VMEM((CZ, FRAMES), jnp.bfloat16),
            pltpu.SemaphoreType.DMA,
            pltpu.SemaphoreType.DMA((4, CHUNKS)),
            pltpu.SemaphoreType.DMA((4, CHUNKS)),
            pltpu.SemaphoreType.DMA((4,)),
            pltpu.SemaphoreType.DMA,
            pltpu.SemaphoreType.DMA,
            pltpu.SemaphoreType.DMA((4,)),
        ],
        compiler_params=pltpu.CompilerParams(
            collective_id=0, has_side_effects=True, vmem_limit_bytes=56 * 2**20
        ),
        name="front",
    )(signal, chosen, wclass, kernel, taps)


def correlate(left, right):
    product = lax.dot_general(
        left.reshape(PANEL, FRAMES), right, (((1,), (1,)), ((), ())), preferred_element_type=jnp.float32
    )
    return product * (1.0 / FRAMES**0.5)


def interleave(h, same, opposite):
    low, high = jnp.where(h == 0, same, opposite), jnp.where(h == 0, opposite, same)
    lane = lax.broadcasted_iota(jnp.int32, (PANEL, 128), 1)
    parts = []
    for i in range(2):
        a, b = low[:, i * 128 : (i + 1) * 128], high[:, i * 128 : (i + 1) * 128]
        parts.append(jnp.where(lane < 64, a, pltpu.roll(b, 64, axis=1)).astype(jnp.bfloat16))
        parts.append(jnp.where(lane < 64, pltpu.roll(a, 64, axis=1), b).astype(jnp.bfloat16))
    return parts


def group_kernel(rows, tiles, own, far_rest, far_part, held, x_out, x_in, z_out, z_in, swap_sem, x_sem, mate_sem, mirror_sem, core_sem, recv_sem, lend_sem, borrow_sem, own_sem):
    loop, slab = lax.axis_index("loop"), lax.axis_index("slab")
    x, z, c = loop // 8, (loop // 2) % 4, loop % 2
    y, h = slab // 2, slab % 2
    z_mate, z_mirror, z_far = z + 1 - 2 * (z % 2), 3 - z, (z + 2) % 4

    def panel(px, pz, pc=None):
        return px * 8 + pz * 2 + (c if pc is None else pc)

    mate, mirror = (panel(x, z_mate), slab), (panel(x, z_mirror), slab)
    across, sibling = (panel(1 - x, z), slab), (panel(x, z, 1 - c), slab)
    inside = [(loop, ((y + dy) % 4) * 2 + h) for dy in (1, 3, 2)]
    outside = [(panel(1 - x, z), ((y + dy) % 4) * 2 + 1 - h) for dy in ORDER]

    barrier = pltpu.get_barrier_semaphore()
    peers = [mate, mirror, across, sibling] + inside + outside
    for peer in peers:
        pl.semaphore_signal(barrier, inc=1, device_id=peer, device_id_type=MESH)
    pl.semaphore_wait(barrier, len(peers))

    def at(p):
        dy = jnp.where(p == 2, 3, jnp.where(p == 3, 2, p))
        return (y + dy) % 4

    def copy(q, py, ph, sem, peer):
        return pltpu.make_async_remote_copy(
            src_ref=held.at[q, py, ph],
            dst_ref=held.at[q, py, ph],
            send_sem=sem.at[q, py, ph],
            recv_sem=recv_sem.at[q, py, ph],
            device_id=peer,
            device_id_type=MESH,
        )

    def copy_far(q, py, sem, peer, src):
        return pltpu.make_async_remote_copy(
            src_ref=src,
            dst_ref=far_rest.at[c, py],
            send_sem=sem.at[q, py, 1 - h],
            recv_sem=recv_sem.at[q, py, 1 - h],
            device_id=peer,
            device_id_type=MESH,
        )

    def arrived(q, py, ph):
        copy(q, py, ph, core_sem, sibling).wait_recv()

    swaps = []
    for i, peer in enumerate(outside + inside):
        to_y, to_h = peer[1] // 2, peer[1] % 2
        swaps.append(pltpu.make_async_remote_copy(
            src_ref=rows.at[to_y, to_h],
            dst_ref=held.at[loop, y, h],
            send_sem=swap_sem.at[i],
            recv_sem=recv_sem.at[loop, y, h],
            device_id=peer,
            device_id_type=MESH,
        ))
    pltpu.make_async_copy(rows.at[y, h], held.at[loop, y, h], recv_sem.at[loop, y, h]).start()
    for i in (0, 4, 1, 5, 2, 6, 3):
        swaps[i].start()

    mine, other = panel(x, z), panel(1 - x, z)

    def own_rest(p):
        py = at(p)
        arrived(mine, py, 1 - h)
        copy(mine, py, 1 - h, mirror_sem, mirror).start()
        copy(mine, py, 1 - h, core_sem, sibling).start()

    def own_first(p):
        py = at(p)
        copy(mine, py, h, mirror_sem, mirror).start()
        copy(mine, py, h, mate_sem, mate).start()
        copy(mine, py, h, core_sem, sibling).start()

    pltpu.make_async_copy(rows.at[y, h], held.at[loop, y, h], recv_sem.at[loop, y, h]).wait()
    copy(mine, y, h, x_sem, across).start()
    own_first(0)

    def straight(p, _):
        arrived(mine, at(p), h)
        own_first(p)

        @pl.when(p == 1)
        def _():
            copy(mine, at(1), h, x_sem, across).start()
        return 0

    lax.fori_loop(1, 3, straight, 0)

    def begin(p, _):
        py = at(p)

        @pl.when(p >= 2)
        def _():
            own_rest(p - 2)
        arrived(other, py, 1 - h)
        copy(other, py, 1 - h, x_sem, across).start()
        copy(other, py, 1 - h, mate_sem, mate).start()
        copy(other, py, 1 - h, core_sem, sibling).start()

        @pl.when(p == 2)
        def _():
            copy(mine, at(2), h, x_sem, across).start()
            arrived(mine, at(3), h)
            own_first(3)
        return 0

    lax.fori_loop(0, 4, begin, 0)
    copy(mine, at(3), h, x_sem, across).start()

    def onward(p, q, odd, rest):
        sem, peer = (mate_sem, mate) if odd else (mirror_sem, mirror)

        @pl.when(p % 2 == odd)
        def _():
            if rest:
                copy_far(q, at(p), sem, peer, held.at[q, at(p), 1 - h]).start()
            else:
                copy(q, at(p), h, sem, peer).start()

    def second(p, _):
        py = at(p)
        for pz, odd in ((z_mirror, 1), (z_mate, 0)):
            q = panel(x, pz)
            arrived(q, py, h)
            onward(p, q, odd, False)
            copy(q, py, h, core_sem, sibling).start()
        return 0

    own_rest(2)
    lax.fori_loop(0, 4, second, 0)
    own_rest(3)

    def rest_to_mate(p, _):
        copy(mine, at(p), 1 - h, mate_sem, mate).start()
        return 0

    lax.fori_loop(0, 4, rest_to_mate, 0)

    def came_across(p, _):
        q = panel(1 - x, z_mate)
        arrived(q, at(p), 1 - h)
        copy(q, at(p), 1 - h, core_sem, sibling).start()
        arrived(other, at(p), h)
        copy(other, at(p), h, core_sem, sibling).start()
        return 0

    lax.fori_loop(0, 4, came_across, 0)

    def from_sibling(px, pz, ph):
        def body(p, _):
            arrived(panel(px, pz, 1 - c), at(p), ph)
            return 0

        lax.fori_loop(0, 4, body, 0)

    def times(q, right):
        return correlate(held[q], right)

    def half(q, ph):
        return held[q, :, ph].reshape(PANEL // 2, FRAMES)

    def lend(axis, j, pc):
        out, into, peer = ((x_out, x_in, across), (z_out, z_in, mirror))[axis]
        return pltpu.make_async_remote_copy(
            src_ref=out.at[j, pc],
            dst_ref=into.at[j, pc],
            send_sem=lend_sem.at[axis, j, pc],
            recv_sem=borrow_sem.at[axis, j, pc],
            device_id=peer,
            device_id_type=MESH,
        )

    def lend_across(j, pz):
        from_sibling(x, pz, h)

        def body(pc, _):
            x_out[j, pc] = times(other, half(panel(x, pz, pc), h)).astype(jnp.bfloat16)
            lend(0, j, pc).start()
            return 0

        lax.fori_loop(0, 2, body, 0)

    def lend_mirror(j, pz):
        from_sibling(1 - x, pz, 1 - h)

        def body(pc, _):
            z_out[j, pc] = times(panel(x, z_mirror), half(panel(1 - x, pz, pc), 1 - h)).astype(jnp.bfloat16)
            lend(1, j, pc).start()
            return 0

        lax.fori_loop(0, 2, body, 0)

    def columns(q, first, width):
        return pl.ds(pl.multiple_of(q * PANEL + first, 128), width)

    def full(px, pz):
        def body(i, _):
            q, j = panel(px, pz, i // 2), i % 2
            right = held[q, pl.ds(2 * j, 2)].reshape(PANEL // 2, FRAMES)
            tiles[:, columns(q, j * 256, 256)] = times(loop, right).astype(jnp.bfloat16)
            return 0

        lax.fori_loop(0, 4, body, 0)

    def place(q, same, opposite):
        for i, part in enumerate(interleave(h, same, opposite)):
            tiles[:, columns(q, i * 128, 128)] = part

    def borrowed(axis, j, pc):
        lend(axis, j, pc).wait_recv()
        return (x_in, z_in)[axis][j, pc].astype(jnp.float32)

    def each_core(body):
        def step(pc, _):
            body(pc)
            return 0

        lax.fori_loop(0, 2, step, 0)

    def early_across(j, _):
        lend_across(j, jnp.where(j == 0, z_mirror, z_mate))
        return 0

    lax.fori_loop(0, 2, early_across, 0)

    def third(p, _):
        q = panel(x, z_mirror)
        arrived(q, at(p), 1 - h)
        onward(p, q, 1, True)
        copy(q, at(p), 1 - h, core_sem, sibling).start()
        return 0

    lax.fori_loop(0, 4, third, 0)

    def to_mirror(j, _):
        lend_mirror(j, jnp.where(j == 0, z, z_mate))
        return 0

    lax.fori_loop(0, 2, to_mirror, 0)

    keep = pltpu.make_async_copy(held.at[loop], own, own_sem)
    keep.start()
    from_sibling(x, z, 0)
    from_sibling(x, z, 1)
    full(x, z)

    def from_far(p, _):
        q = panel(x, z_far)
        arrived(q, at(p), h)
        copy(q, at(p), h, core_sem, sibling).start()
        return 0

    lax.fori_loop(0, 4, from_far, 0)
    lend_across(2, z_far)
    from_sibling(1 - x, z, h)
    full(1 - x, z)

    def fourth(p, _):
        q = panel(x, z_mate)
        arrived(q, at(p), 1 - h)
        onward(p, q, 0, True)
        copy(q, at(p), 1 - h, core_sem, sibling).start()
        return 0

    lax.fori_loop(0, 4, fourth, 0)

    from_sibling(x, z_mirror, 1 - h)
    from_sibling(x, z_mate, 1 - h)

    def whole(i, _):
        full(x, jnp.where(i == 0, z_mirror, z_mate))
        return 0

    lax.fori_loop(0, 2, whole, 0)

    def part_mate(pc):
        q = panel(1 - x, z_mate, pc)
        place(q, borrowed(0, 1, pc), times(loop, half(q, 1 - h)))

    def none_mirror(pc):
        place(panel(1 - x, z_mirror, pc), borrowed(0, 0, pc), borrowed(1, 0, pc))

    def none_far(pc):
        place(panel(1 - x, z_far, pc), borrowed(0, 2, pc), borrowed(1, 1, pc))

    def first_far(pc):
        far_part[pc] = times(loop, half(panel(x, z_far, pc), h)).astype(jnp.bfloat16)

    each_core(part_mate)
    each_core(first_far)
    each_core(none_mirror)

    def fifth(p, _):
        q = panel(x, z_far)
        arrived(q, at(p), 1 - h)
        copy_far(q, at(p), core_sem, sibling, far_rest.at[c, at(p)]).start()
        return 0

    lax.fori_loop(0, 4, fifth, 0)
    each_core(none_far)

    from_sibling(x, z_far, 1 - h)

    keep.wait()
    for swap in swaps:
        swap.wait_send()
    for axis, count in ((0, 3), (1, 2)):
        for j in range(count):
            for pc in range(2):
                lend(axis, j, pc).wait_send()

    def left(p, _):
        py = at(p)
        for q, ph in ((mine, h), (mine, 1 - h), (other, 1 - h)):
            copy(q, py, ph, mate_sem, mate).wait_send()
        for q, ph in ((mine, h), (mine, 1 - h)):
            copy(q, py, ph, mirror_sem, mirror).wait_send()
        for q, ph in ((mine, h), (other, 1 - h)):
            copy(q, py, ph, x_sem, across).wait_send()

        for ph in range(2):
            @pl.when(p % 2 == 1)
            def _():
                copy(panel(x, z_mirror), py, ph, mate_sem, mate).wait_send()

            @pl.when(p % 2 == 0)
            def _():
                copy(panel(x, z_mate), py, ph, mirror_sem, mirror).wait_send()
            for q in (mine, other, panel(x, z_mate), panel(x, z_mirror)):
                copy(q, py, ph, core_sem, sibling).wait_send()
        copy(panel(x, z_far), py, h, core_sem, sibling).wait_send()
        copy_far(panel(x, z_far), py, core_sem, sibling, far_rest.at[c, py]).wait_send()
        copy(panel(1 - x, z_mate), py, 1 - h, core_sem, sibling).wait_send()
        return 0

    lax.fori_loop(0, 4, left, 0)


def group(rows):
    block = (N_LOOP, 4, 2)
    part = (2, PANEL, PANEL // 2)
    return pl.pallas_call(
        group_kernel,
        out_shape=(
            pltpu.VMEM((PANEL, N_LOOP * PANEL), jnp.bfloat16),
            pltpu.VMEM((4, 2, SHARE, FRAMES), jnp.bfloat16),
            pltpu.VMEM((2, 4, SHARE, FRAMES), jnp.bfloat16),
            pltpu.VMEM(part, jnp.bfloat16),
        ),
        in_specs=[pl.BlockSpec(memory_space=pl.ANY)],
        out_specs=(pl.BlockSpec(memory_space=pltpu.VMEM),) * 4,
        scratch_shapes=[pltpu.VMEM(block + (SHARE, FRAMES), jnp.bfloat16)]
        + [pltpu.VMEM((count,) + part, jnp.bfloat16) for count in (3, 3, 2, 2)]
        + [pltpu.SemaphoreType.DMA((7,))]
        + [pltpu.SemaphoreType.DMA(block)] * 5
        + [pltpu.SemaphoreType.DMA((2, 3, 2))] * 2
        + [pltpu.SemaphoreType.DMA],
        compiler_params=pltpu.CompilerParams(
            collective_id=1, has_side_effects=True, vmem_limit_bytes=40 * 2**20
        ),
        name="group",
    )(pltpu.with_memory_space_constraint(rows, pltpu.VMEM))


def finish_kernel(tiles, own, far_rest, far_part, out, stage, sems):
    loop, h = lax.axis_index("loop"), lax.axis_index("slab") % 2
    far = loop // 8 * 4 + (loop // 2 + 2) % 4
    wide = 2 * PANEL

    def columns(pair):
        return pl.ds(pl.multiple_of(pair * wide, wide), wide)

    def ready(i):
        pair = (far + 1 + i) % 8
        return pltpu.make_async_copy(tiles.at[:, columns(pair)], out.at[:, columns(pair)], sems.at[i])

    for i in range(7):
        ready(i).start()

    def body(pc, _):
        right = far_rest[pc].reshape(PANEL // 2, FRAMES)
        parts = interleave(h, far_part[pc].astype(jnp.float32), correlate(own[...], right))
        for i, part in enumerate(parts):
            stage[:, pl.ds(pl.multiple_of(pc * PANEL + i * 128, 128), 128)] = part
        return 0

    lax.fori_loop(0, 2, body, 0)
    last = pltpu.make_async_copy(stage, out.at[:, columns(far)], sems.at[7])
    last.start()
    for i in range(7):
        ready(i).wait()
    last.wait()


def finish(tiles, own, far_rest, far_part):
    return pl.pallas_call(
        finish_kernel,
        out_shape=jax.ShapeDtypeStruct((PANEL, N_LOOP * PANEL), jnp.bfloat16),
        in_specs=[pl.BlockSpec(memory_space=pl.ANY)] + [pl.BlockSpec(memory_space=pltpu.VMEM)] * 3,
        out_specs=pl.BlockSpec(memory_space=pl.ANY),
        scratch_shapes=[pltpu.VMEM((PANEL, 2 * PANEL), jnp.bfloat16), pltpu.SemaphoreType.DMA((8,))],
        compiler_params=pltpu.CompilerParams(vmem_limit_bytes=12 * 2**20),
        name="finish",
    )(*(pltpu.with_memory_space_constraint(array, pltpu.VMEM) for array in (tiles, own, far_rest, far_part)))


def local(signal, width_class, kernel, taps, chosen):
    rows = front(signal, chosen.reshape(1, PANEL), width_class.reshape(CX * CY, CZ), kernel, taps)
    wide = finish(*group(rows.reshape(4, 2, SHARE, FRAMES)))
    return wide.reshape(PANEL, 1, N_LOOP * PANEL)


def solution(mesh):
    in_specs = (
        P("slab", "loop", None, None),
        P("slab", "loop", None),
        P(),
        P(),
        P("loop", "slab", None),
    )
    return jax.shard_map(local, mesh=mesh, in_specs=in_specs, out_specs=P("loop", "slab", None), check_vma=False)
```
